32 devices in a mesh: dp: 4 (over y, core), expert: 8 (over z, x).
Axes of the slice: x: 2, y: 2, z: 4, core: 2. Of those that a mesh axis runs over, the one named last changes fastest.
Arguments:
- tokens: bfloat16 [4096, 5120], P(('dp', 'expert')), may hold values from -6 to 6
- grad_out: bfloat16 [4096, 5120], P(('dp', 'expert')), may hold values from -1.5 to 1.5
- expert_ids: int32 [4096, 2], P(('dp', 'expert')), may hold values from 0 to 7, as said below
- gate_codes: int32 [4096, 2], P(('dp', 'expert')), may hold values from 1 to 1023
- w_up: bfloat16 [8, 5120, 768], P('expert', 'dp'), may hold values from -0.078125 to 0.078125
- w_down: bfloat16 [8, 5120, 768], P('expert', 'dp'), may hold values from -2.5 to 2.5
Outputs:
- layer_output: bfloat16 [4096, 5120], P(('dp', 'expert'))
- grad_tokens: bfloat16 [4096, 5120], P(('dp', 'expert'))
- grad_up: bfloat16 [8, 5120, 768], P('expert', 'dp')
- grad_down: bfloat16 [8, 5120, 768], P('expert', 'dp')
The draws below stay inside these ranges and needn't reach their ends.
Inputs may be any that keep to these rules, and one draw needn't show every extreme that they name: `expert_ids`: each row names two different experts. Among the rows of one device no expert is named more than 38 times, and in every draw one expert is named exactly 38 times by the rows of every device.
All inputs are finite; a program needn't handle non-finite values.
Results may differ from the reference program's by a relative error of at most 0.0065.
Values may be sent and summed in bfloat16 or wider, within the bound.
No kernel may reach another device: no remote copies, remote signals or barrier semaphores. Data moves between devices by JAX's collectives and lax.ppermute only.
A program may use at most 192 MiB of HBM per device.

```python
import math
import jax
import jax.numpy as jnp
from jax import lax

D = 5120
H = 768
LAYERS = 40
TOK_DEV = 128
EXPERTS = 8
TOKENS = 4096
CAP = 38
N_DP = 4
N_EXPERT = 8


def draw_expert_ids(key, part):
    block_count = TOKENS // TOK_DEV
    hot_expert = jax.random.randint(jax.random.fold_in(key, 7), (), 0, EXPERTS).astype(jnp.int32)
    unit_count = (EXPERTS - 1) * CAP
    drop_count = EXPERTS * CAP - 2 * TOK_DEV
    kept_total = 2 * TOK_DEV - CAP

    def one_block(block_index):
        block_key = jax.random.fold_in(key, block_index)
        unit_ranks = jax.random.permutation(jax.random.fold_in(block_key, 1), unit_count)
        kept = unit_ranks >= drop_count
        chosen = jnp.nonzero(kept, size=kept_total, fill_value=0)[0].astype(jnp.int32)
        others = (chosen // CAP).astype(jnp.int32)
        others = others + (others >= hot_expert).astype(jnp.int32)
        entries = jnp.concatenate([jnp.full((CAP,), 1, jnp.int32) * hot_expert, others])
        paired = jnp.stack([entries[:TOK_DEV], entries[TOK_DEV:]], axis=1)
        row_order = jax.random.permutation(jax.random.fold_in(block_key, 2), TOK_DEV)
        return paired[row_order]
    return jax.vmap(one_block)(jnp.arange(block_count, dtype=jnp.int32)).reshape(TOKENS, 2)


def set_ends(values, stream_key, smallest, high):
    longest = values.shape.index(max(values.shape))
    spots = []
    for shift in (0, 1):
        where = [jax.random.randint(jax.random.fold_in(stream_key, axis), (), 0, length) for axis, length in enumerate(values.shape)]
        where[longest] = (where[longest] + shift) % values.shape[longest]
        spots.append(tuple(where))
    return values.at[spots[0]].set(smallest).at[spots[1]].set(high)


def steps_of(stream_key, shape, cuts, smallest, top_value):
    def one(dim, blocks):
        draws = jax.random.uniform(jax.random.fold_in(jax.random.fold_in(stream_key, 6), dim), (blocks,), jnp.float32, smallest / len(cuts), top_value / len(cuts))
        return jnp.repeat(jnp.exp(draws), shape[dim] // blocks).reshape((-1,) + (1,) * (len(shape) - dim - 1))

    level = one(*cuts[0])
    for cut in cuts[1:]:
        level = level * one(*cut)
    return level


def noise(rng, extent, width, bound, split=(), kind=jnp.bfloat16):
    drawn = width * jax.random.normal(rng, extent, jnp.float32)
    if split:
        drawn = drawn * steps_of(rng, extent, split, -0.22, 0.18)
    return jnp.clip(drawn, -bound, bound).astype(kind)


def setup_inputs(seed: int = 0) -> dict:
    splits = jax.random.split(jax.random.key(seed), 7)
    tokens = noise(splits[0], (TOKENS, D), 1.0, 6.0, ((0, 32),))
    grad_out = noise(splits[1], (TOKENS, D), 0.25, 1.5, ((0, 32),))
    expert_ids = draw_expert_ids(jax.random.fold_in(splits[6], 71), 0)
    gate_codes = set_ends(jax.random.randint(splits[3], (TOKENS, 2), 1, 1024), jax.random.fold_in(splits[3], 1), 1, 1023).astype(jnp.int32)
    w_up = noise(splits[4], (EXPERTS, D, H), D ** -0.5, 0.078125, ((0, 8), (1, 4)))
    w_down = noise(splits[5], (EXPERTS, D, H), (max(1, H // 128)) ** -0.5, 2.5, ((0, 8), (1, 4)))
    return dict(tokens=tokens, grad_out=grad_out, expert_ids=expert_ids, gate_codes=gate_codes, w_up=w_up, w_down=w_down)


def activate(values):
    return jax.nn.gelu(values, approximate=True)

def contract_rows(former, latter):
    return lax.dot_general(former, latter, (((0,), (0,)), ((), ())), preferred_element_type=jnp.float32)

def contract_columns(former, latter):
    return lax.dot_general(former, latter, (((1,), (1,)), ((), ())), preferred_element_type=jnp.float32)

def reference(tokens, grad_out, expert_ids, gate_codes, w_up, w_down):
    out_scale = 1.0 / math.sqrt(2.0 * LAYERS)
    gate_values = gate_codes.astype(jnp.float32)
    flat_gates = (gate_values / lax.optimization_barrier(jnp.sum(gate_values, axis=1, keepdims=True))).reshape(-1)
    flat_ids = expert_ids.reshape(-1)
    flat_rows = (jnp.arange(2 * TOKENS, dtype=jnp.int32) // 2).astype(jnp.int32)
    most_rows = N_DP * N_EXPERT * CAP

    def one_expert(running, inputs):
        mixed_sum, input_sum = running
        expert_index, up_weight, down_weight = inputs
        matches = flat_ids == expert_index
        picked = jnp.nonzero(matches, size=most_rows, fill_value=0)[0].astype(jnp.int32)
        live_slot = jnp.arange(most_rows, dtype=jnp.int32) < jnp.sum(matches.astype(jnp.int32))
        token_rows = flat_rows[picked]
        weights = jnp.where(live_slot, flat_gates[picked], jnp.zeros((), flat_gates.dtype))
        inputs_here = jnp.where(live_slot[:, None], tokens[token_rows], jnp.zeros((), tokens.dtype))
        slot_grads = (out_scale * weights[:, None] * grad_out[token_rows].astype(jnp.float32)).astype(jnp.bfloat16)
        pre_act = jnp.dot(inputs_here, up_weight, preferred_element_type=jnp.float32)
        hidden = activate(pre_act).astype(jnp.bfloat16)
        expert_out = contract_columns(hidden, down_weight).astype(jnp.bfloat16)
        hidden_grad = jnp.dot(slot_grads, down_weight, preferred_element_type=jnp.float32)
        pre_grad = jax.vjp(activate, pre_act)[1](hidden_grad)[0].astype(jnp.bfloat16)
        row_grad = contract_columns(pre_grad, up_weight).astype(jnp.bfloat16)
        up_grad = contract_rows(inputs_here, pre_grad).astype(jnp.bfloat16)
        down_grad = contract_rows(slot_grads, hidden).astype(jnp.bfloat16)
        mixed_sum = mixed_sum.at[token_rows].add(out_scale * weights[:, None] * expert_out.astype(jnp.float32))
        input_sum = input_sum.at[token_rows].add(row_grad.astype(jnp.float32))
        return ((mixed_sum, input_sum), (up_grad, down_grad))
    initial = (jnp.zeros((TOKENS, D), jnp.float32), jnp.zeros((TOKENS, D), jnp.float32))
    (mixed_sum, input_sum), (grad_up, grad_down) = lax.scan(one_expert, initial, (jnp.arange(EXPERTS, dtype=jnp.int32), w_up, w_down))
    return (mixed_sum.astype(jnp.bfloat16), input_sum.astype(jnp.bfloat16), grad_up, grad_down)
```

```python
import math

import jax
import jax.numpy as jnp
from jax import lax
from jax.sharding import PartitionSpec as P

LAYERS = 40
ROW_TILE = 8


def activate(values):
    return jax.nn.gelu(values, approximate=True)


def contract_rows(former, latter):
    return lax.dot_general(
        former, latter, (((0,), (0,)), ((), ())), preferred_element_type=jnp.float32
    )


def contract_columns(former, latter):
    return lax.dot_general(
        former, latter, (((1,), (1,)), ((), ())), preferred_element_type=jnp.float32
    )


def permute_xor(values, axis, mask):
    size = lax.axis_size(axis)
    return lax.ppermute(values, axis, [(i, i ^ mask) for i in range(size)])


def plan_slots(routing, experts, block):
    n_rows = routing.shape[0]
    ids = routing[:, :2]
    codes = routing[:, 2:].astype(jnp.float32)
    gates = codes / jnp.sum(codes, axis=1, keepdims=True)
    match = ids[:, :, None] == experts[None, None, :]
    named = jnp.any(match, axis=1)
    order = jnp.arange(n_rows, dtype=jnp.int32)
    earlier = (order[None, :] < order[:, None]).astype(jnp.bfloat16)
    before = jnp.dot(earlier, named.astype(jnp.bfloat16), preferred_element_type=jnp.float32)
    place = before.astype(jnp.int32)[:, :, None] == jnp.arange(block, dtype=jnp.int32)
    picks = [
        (match[:, k, :, None] & place).reshape(n_rows, experts.shape[0] * block) for k in (0, 1)
    ]
    either = (picks[0] | picks[1]).astype(jnp.bfloat16)
    slot_gates = jnp.sum(
        jnp.where(picks[0], gates[:, :1], 0.0) + jnp.where(picks[1], gates[:, 1:], 0.0), axis=0
    )
    return [pick.astype(jnp.bfloat16) for pick in picks], either, gates, slot_gates


def exchange(blocks, n_group, block):
    parts = [blocks[:block]]
    for k in range(1, n_group):
        parts.append(permute_xor(blocks[k * block : (k + 1) * block], "expert", k))
    return jnp.concatenate(parts, axis=0)


def spread_columns(rows):
    n_dp = lax.axis_size("dp")
    me = lax.axis_index("dp")
    width = rows.shape[1] // n_dp
    parts = []
    for k in range(n_dp):
        piece = lax.dynamic_slice(rows, (0, (me ^ k) * width), (rows.shape[0], width))
        parts.append(permute_xor(piece, "dp", k) if k else piece)
    return jnp.concatenate(parts, axis=0)


def gather_rows(rows):
    n_dp = lax.axis_size("dp")
    return jnp.concatenate(
        [rows] + [permute_xor(rows, "dp", k) for k in range(1, n_dp)], axis=0
    )


def local(tokens, grad_out, expert_ids, gate_codes, w_up, w_down):
    n_expert = lax.axis_size("expert")
    n_rows = tokens.shape[0]
    capacity = max(2, 12 * n_rows // (5 * n_expert))
    block = -(-capacity // ROW_TILE) * ROW_TILE
    half = n_expert // 2
    out_scale = 1.0 / math.sqrt(2.0 * LAYERS)
    me = lax.axis_index("expert")
    experts = me ^ jnp.arange(half, dtype=jnp.int32)

    routing = jnp.concatenate([expert_ids, gate_codes], axis=1)
    far_routing = permute_xor(routing, "expert", half)
    far_tokens = permute_xor(tokens, "expert", half)
    far_grads = permute_xor(grad_out, "expert", half)
    up_weight = lax.all_gather(w_up, "dp", axis=1, tiled=True)[0]
    down_weight = lax.all_gather(w_down, "dp", axis=1, tiled=True)[0]

    plans = [plan_slots(routing, experts, block), plan_slots(far_routing, experts, block)]

    def dispatch_rows(plan, rows):
        return exchange(contract_rows(plan[1], rows).astype(jnp.bfloat16), half, block)

    def dispatch_grads(plan, grads):
        picked = contract_rows(plan[1], grads)
        scaled = (out_scale * plan[3])[:, None] * picked
        return exchange(scaled.astype(jnp.bfloat16), half, block)

    def combine_out(plan, back):
        first, second = (
            jnp.dot(pick, back, preferred_element_type=jnp.float32) for pick in plan[0]
        )
        weights = out_scale * plan[2]
        return weights[:, :1] * first + weights[:, 1:] * second

    def combine_grad(plan, back):
        return jnp.dot(plan[1], back, preferred_element_type=jnp.float32)

    rows, grads, hiddens, pre_grads, outs, row_grads = [], [], [], [], [], []
    for plan, token_rows, cotangents in zip(plans, (tokens, far_tokens), (grad_out, far_grads)):
        recv_rows = dispatch_rows(plan, token_rows)
        recv_grads = dispatch_grads(plan, cotangents)
        pre_act = jnp.dot(recv_rows, up_weight, preferred_element_type=jnp.float32)
        hidden = activate(pre_act).astype(jnp.bfloat16)
        expert_out = contract_columns(hidden, down_weight).astype(jnp.bfloat16)
        outs.append(exchange(expert_out, half, block))
        hidden_grad = jnp.dot(recv_grads, down_weight, preferred_element_type=jnp.float32)
        pre_grad = jax.vjp(activate, pre_act)[1](hidden_grad)[0].astype(jnp.bfloat16)
        row_grad = contract_columns(pre_grad, up_weight).astype(jnp.bfloat16)
        row_grads.append(exchange(row_grad, half, block))
        rows.append(recv_rows)
        grads.append(recv_grads)
        hiddens.append(hidden)
        pre_grads.append(pre_grad)

    far_out = permute_xor(combine_out(plans[1], outs[1]).astype(jnp.bfloat16), "expert", half)
    layer_output = (combine_out(plans[0], outs[0]) + far_out.astype(jnp.float32)).astype(
        jnp.bfloat16
    )
    far_grad = permute_xor(
        combine_grad(plans[1], row_grads[1]).astype(jnp.bfloat16), "expert", half
    )
    grad_tokens = (combine_grad(plans[0], row_grads[0]) + far_grad.astype(jnp.float32)).astype(
        jnp.bfloat16
    )

    join = lambda parts: jnp.concatenate(parts, axis=0)
    up_sum = contract_rows(spread_columns(join(rows)), gather_rows(join(pre_grads)))
    down_sum = contract_rows(spread_columns(join(grads)), gather_rows(join(hiddens)))
    grad_up = up_sum.astype(jnp.bfloat16)[None]
    grad_down = down_sum.astype(jnp.bfloat16)[None]
    return (layer_output, grad_tokens, grad_up, grad_down)


def solution(mesh):
    in_specs = (
        P(("dp", "expert"), None),
        P(("dp", "expert"), None),
        P(("dp", "expert"), None),
        P(("dp", "expert"), None),
        P("expert", "dp", None),
        P("expert", "dp", None),
    )
    out_specs = (
        P(("dp", "expert"), None),
        P(("dp", "expert"), None),
        P("expert", "dp", None),
        P("expert", "dp", None),
    )
    return jax.shard_map(local, mesh=mesh, in_specs=in_specs, out_specs=out_specs, check_vma=False)
```

```python
import functools
import math

import jax
import jax.numpy as jnp
from jax import lax
from jax.experimental import pallas as pl
from jax.experimental.pallas import tpu as pltpu
from jax.sharding import PartitionSpec as P

LAYERS = 40
OUT_SCALE = 1.0 / math.sqrt(2.0 * LAYERS)
ROW_TILE = 8
VMEM_LIMIT = 60 * 1024 * 1024
F32, BF16, I32 = jnp.float32, jnp.bfloat16, jnp.int32
GELU_SCALE = math.sqrt(2.0 / math.pi)
GELU_CUBE = 0.044715


def dot(former, latter):
    return jnp.dot(former, latter, preferred_element_type=F32)


def contract_rows(former, latter):
    return lax.dot_general(former, latter, (((0,), (0,)), ((), ())), preferred_element_type=F32)


def contract_columns(former, latter):
    return lax.dot_general(former, latter, (((1,), (1,)), ((), ())), preferred_element_type=F32)


def iota(shape, dim):
    return lax.broadcasted_iota(I32, shape, dim)


def as_bf16(condition):
    return jnp.where(condition, 1.0, 0.0).astype(BF16)


def gelu(v):
    t = jnp.tanh(GELU_SCALE * (v + GELU_CUBE * (v * v * v)))
    return v * (0.5 * (1.0 + t))


def gelu_slope(v):
    t = jnp.tanh(GELU_SCALE * (v + GELU_CUBE * (v * v * v)))
    inner = GELU_SCALE * (1.0 + 3.0 * GELU_CUBE * (v * v))
    return 0.5 * (1.0 + t) + 0.5 * v * (1.0 - t * t) * inner


def stack(pieces):
    return jnp.concatenate([piece.astype(F32) for piece in pieces], axis=0).astype(BF16)


SHORT = pl.CostEstimate(flops=1, bytes_accessed=1, transcendentals=0)


def params(**kwargs):
    return pltpu.CompilerParams(vmem_limit_bytes=VMEM_LIMIT, **kwargs)


def slots_by_row(routing_t, me, half, block):
    n_rows = routing_t.shape[1]
    ids = [routing_t[k : k + 1, :] for k in (0, 1)]
    codes = [routing_t[k : k + 1, :].astype(F32) for k in (2, 3)]
    total = codes[0] + codes[1]
    gates = [code / total for code in codes]
    height = -(-half // 8) * 8
    expert = me ^ iota((height, n_rows), 0)
    named = [ids[k] == expert for k in (0, 1)]
    either = named[0] | named[1]
    earlier = as_bf16(iota((n_rows, n_rows), 0) < iota((n_rows, n_rows), 1))
    before = dot(as_bf16(either), earlier)
    before = jnp.where(either, before, -1.0)
    gate = jnp.where(named[0], gates[0], jnp.where(named[1], gates[1], 0.0))
    place = iota((block, n_rows), 0).astype(F32)
    hot = [jnp.where(place == before[k : k + 1, :], 1.0, 0.0) for k in range(half)]
    slot_gates = [
        jnp.sum(hot[k] * gate[k : k + 1, :], axis=1, keepdims=True) for k in range(half)
    ]
    return jnp.concatenate(hot, axis=0).astype(BF16), jnp.concatenate(slot_gates, axis=0)


def slots_by_column(routing, me, half, block):
    n_rows = routing.shape[0]
    n_slots = half * block
    ids = [routing[:, k : k + 1] for k in (0, 1)]
    codes = [routing[:, k : k + 1].astype(F32) for k in (2, 3)]
    total = codes[0] + codes[1]
    gates = [code / total for code in codes]
    lanes = 128
    expert = me ^ iota((n_rows, lanes), 1)
    within = iota((n_rows, lanes), 1) < half
    either = ((ids[0] == expert) | (ids[1] == expert)) & within
    earlier = as_bf16(iota((n_rows, n_rows), 1) < iota((n_rows, n_rows), 0))
    before = dot(earlier, as_bf16(either))
    slot = iota((lanes, n_slots), 1)
    owner = iota((lanes, n_slots), 0)
    spread = as_bf16((slot >= owner * block) & (slot < (owner + 1) * block))
    before = dot(before.astype(BF16), spread)
    number = dot(as_bf16(iota((n_rows, lanes), 1) >= 0), as_bf16(slot >= (owner + 1) * block))
    slot_row = iota((n_rows, n_slots), 1)
    owner_row = number.astype(I32)
    place = (slot_row - owner_row * block).astype(F32) == before
    slot_expert = me ^ owner_row
    hot = [as_bf16((ids[k] == slot_expert) & place) for k in (0, 1)]
    return hot, gates


def dispatch_kernel(groups, block, gated, n_after, me_ref, routing_ref, *refs):
    source = refs[0]
    out_ref, hot_ref, gate_ref = refs[1 + n_after :]

    @pl.when(pl.program_id(0) == 0)
    def _():
        hot, gate = slots_by_row(routing_ref[...], me_ref[0], groups, block)
        hot_ref[...] = hot
        gate_ref[...] = jnp.broadcast_to(gate, gate_ref.shape)

    rows = dot(hot_ref[...], source[...])
    if gated:
        rows = (OUT_SCALE * gate_ref[:, :1]) * rows
    for k in range(groups):
        out_ref[k] = rows[k * block : (k + 1) * block].astype(BF16)


def dispatch(me, routing_t, source, groups, block, chunk, gated=False, wait_for=()):
    n_rows, width = source.shape
    return pl.pallas_call(
        functools.partial(dispatch_kernel, groups, block, gated, len(wait_for)),
        grid_spec=pltpu.PrefetchScalarGridSpec(
            num_scalar_prefetch=1,
            grid=(width // chunk,),
            in_specs=[
                pl.BlockSpec(routing_t.shape, lambda d, me: (0, 0)),
                pl.BlockSpec((n_rows, chunk), lambda d, me: (0, d)),
            ]
            + [pl.BlockSpec(memory_space=pl.ANY) for _ in wait_for],
            out_specs=pl.BlockSpec((groups, block, chunk), lambda d, me: (0, 0, d)),
            scratch_shapes=[
                pltpu.VMEM((groups * block, n_rows), BF16),
                pltpu.VMEM((groups * block, 128), F32),
            ],
        ),
        out_shape=jax.ShapeDtypeStruct((groups, block, width), BF16),
        compiler_params=params(),
        cost_estimate=SHORT,
        name="dispatch",
    )(me, routing_t, source, *wait_for)


def forward_kernel(n, block, n_chunks, me_ref, rows_ref, up_ref, down_ref, *refs):
    outs = refs[:n]
    sent_ref, hidden_ref, pre_ref = refs[n:]
    step = pl.program_id(0)

    @pl.when(step < n_chunks)
    def _():
        rows = stack([rows_ref[me_ref[0] ^ k] for k in range(n)])
        sent_ref[0] = rows
        part = dot(rows, up_ref[...])

        @pl.when(step == 0)
        def _():
            pre_ref[...] = part

        @pl.when(step > 0)
        def _():
            pre_ref[...] += part

        @pl.when(step == n_chunks - 1)
        def _():
            hidden_ref[...] = gelu(pre_ref[...]).astype(BF16)

    @pl.when(step >= n_chunks)
    def _():
        rows = contract_columns(hidden_ref[...], down_ref[...])
        for k in range(n):
            outs[k][...] = rows[k * block : (k + 1) * block].astype(BF16)


def forward(me, rows_in, up_weight, down_weight, n_chunks):
    n, block, width = rows_in.shape
    hidden = up_weight.shape[1]
    chunk = width // n_chunks
    rows = n * block
    early = lambda i: jnp.minimum(i, n_chunks - 1)
    late = lambda i: jnp.maximum(i - n_chunks, 0)
    whole = pl.BlockSpec((rows, hidden), lambda i, me: (0, 0))
    results = pl.pallas_call(
        functools.partial(forward_kernel, n, block, n_chunks),
        grid_spec=pltpu.PrefetchScalarGridSpec(
            num_scalar_prefetch=1,
            grid=(2 * n_chunks,),
            in_specs=[
                pl.BlockSpec((n, block, chunk), lambda i, me: (0, 0, early(i))),
                pl.BlockSpec((chunk, hidden), lambda i, me: (early(i), 0)),
                pl.BlockSpec((chunk, hidden), lambda i, me: (late(i), 0)),
            ],
            out_specs=[
                pl.BlockSpec((block, chunk), lambda i, me: (0, late(i))) for _ in range(n)
            ]
            + [pl.BlockSpec((1, rows, chunk), lambda i, me: (early(i), 0, 0)), whole, whole],
        ),
        out_shape=[jax.ShapeDtypeStruct((block, width), BF16) for _ in range(n)]
        + [
            jax.ShapeDtypeStruct((n_chunks, 2 * rows, chunk), BF16),
            jax.ShapeDtypeStruct((rows, hidden), BF16),
            jax.ShapeDtypeStruct((rows, hidden), F32),
        ],
        compiler_params=params(),
        cost_estimate=SHORT,
        name="expert_forward",
    )(me, rows_in, up_weight, down_weight)
    return (results[:n],) + tuple(results[n:])


def backward_kernel(n, block, n_chunks, me_ref, grads_ref, down_ref, up_ref, pre_ref, *refs):
    carried = refs[: n // 2]
    outs = refs[n // 2 + 2 : -3]
    sent_ref, middle_ref, sum_ref = refs[-3:]
    step = pl.program_id(0)
    half = n // 2

    @pl.when(step < n_chunks)
    def _():
        rows = stack([grads_ref[me_ref[0] ^ k] for k in range(n)])
        sent_ref[0] = rows
        part = dot(rows, down_ref[...])

        @pl.when(step == 0)
        def _():
            sum_ref[...] = part

        @pl.when(step > 0)
        def _():
            sum_ref[...] += part

        @pl.when(step == n_chunks - 1)
        def _():
            middle_ref[...] = (sum_ref[...] * gelu_slope(pre_ref[...])).astype(BF16)

    @pl.when(step >= n_chunks)
    def _():
        rows = contract_columns(middle_ref[...], up_ref[...])
        for k in range(n):
            piece = rows[k * block : (k + 1) * block]
            if k < half:
                piece = jnp.concatenate([carried[k][...].astype(F32), piece], axis=0)
            outs[k][...] = piece.astype(BF16)


def backward(me, grads, pre_act, down_weight, up_weight, n_chunks, carried, sent, wait_for):
    n, block, width = grads.shape
    half = n // 2
    chunk = width // n_chunks
    rows = n * block
    hidden = up_weight.shape[1]
    early = lambda i: jnp.minimum(i, n_chunks - 1)
    late = lambda i: jnp.maximum(i - n_chunks, 0)
    whole = pl.BlockSpec((rows, hidden), lambda i, me: (0, 0))
    depths = [2 * block if k < half else block for k in range(n)]
    results = pl.pallas_call(
        functools.partial(backward_kernel, n, block, n_chunks),
        grid_spec=pltpu.PrefetchScalarGridSpec(
            num_scalar_prefetch=1,
            grid=(2 * n_chunks,),
            in_specs=[
                pl.BlockSpec((n, block, chunk), lambda i, me: (0, 0, early(i))),
                pl.BlockSpec((chunk, hidden), lambda i, me: (early(i), 0)),
                pl.BlockSpec((chunk, hidden), lambda i, me: (late(i), 0)),
                whole,
            ]
            + [pl.BlockSpec((block, chunk), lambda i, me: (0, late(i))) for _ in carried]
            + [pl.BlockSpec(memory_space=pl.ANY)] * 2,
            out_specs=[
                pl.BlockSpec((depth, chunk), lambda i, me: (0, late(i))) for depth in depths
            ]
            + [
                pl.BlockSpec((1, rows, chunk), lambda i, me: (early(i), 1, 0)),
                whole,
            ],
            scratch_shapes=[pltpu.VMEM((rows, hidden), F32)],
        ),
        out_shape=[jax.ShapeDtypeStruct((depth, width), BF16) for depth in depths]
        + [
            jax.ShapeDtypeStruct(sent.shape, BF16),
            jax.ShapeDtypeStruct((rows, hidden), BF16),
        ],
        input_output_aliases={5 + len(carried): n},
        compiler_params=params(),
        cost_estimate=SHORT,
        name="expert_backward",
    )(me, grads, down_weight, up_weight, pre_act, *carried, sent, wait_for)
    return results[:half], results[half:n], results[n], results[n + 1]


def combine_kernel(groups, block, offset, gated, n_arrived, n_after, me_ref, routing_ref, *refs):
    n_blocks = groups
    blocks = refs[:n_blocks]
    arrived = refs[n_blocks : n_blocks + n_arrived]
    outs = refs[n_blocks + n_arrived + n_after : -3]
    hot_refs = refs[-3:-1]
    gate_ref = refs[-1]

    @pl.when(pl.program_id(0) == 0)
    def _():
        hot, gates = slots_by_column(routing_ref[...], me_ref[0], groups, block)
        if gated:
            for k in (0, 1):
                hot_refs[k][...] = hot[k]
                gate_ref[:, k * 128 : (k + 1) * 128] = jnp.broadcast_to(
                    OUT_SCALE * gates[k], (gates[k].shape[0], 128)
                )
        else:
            hot_refs[0][...] = (hot[0].astype(F32) + hot[1].astype(F32)).astype(BF16)

    rows = stack([ref[...].astype(F32)[offset : offset + block] for ref in blocks])
    total = dot(hot_refs[0][...], rows)
    if gated:
        total = gate_ref[:, :1] * total + gate_ref[:, 128:129] * dot(hot_refs[1][...], rows)
    if arrived:
        total = total + jnp.concatenate([ref[...].astype(F32) for ref in arrived], axis=0)
    at = 0
    for ref in outs:
        ref[...] = total[at : at + ref.shape[0]].astype(BF16)
        at += ref.shape[0]


def combine(
    me, routing, blocks, block, chunk, gated=False, offset=0, arrived=(), wait_for=(), parts=None
):
    n_rows = routing.shape[0]
    groups = len(blocks)
    depth, width = blocks[0].shape
    by_rows = lambda n: pl.BlockSpec((n, chunk), lambda d, me: (0, d))
    results = pl.pallas_call(
        functools.partial(
            combine_kernel, groups, block, offset, gated, len(arrived), len(wait_for)
        ),
        grid_spec=pltpu.PrefetchScalarGridSpec(
            num_scalar_prefetch=1,
            grid=(width // chunk,),
            in_specs=[pl.BlockSpec(routing.shape, lambda d, me: (0, 0))]
            + [by_rows(depth) for _ in blocks]
            + [by_rows(part.shape[0]) for part in arrived]
            + [pl.BlockSpec(memory_space=pl.ANY) for _ in wait_for],
            out_specs=[by_rows(n) for n in parts or (n_rows,)],
            scratch_shapes=[
                pltpu.VMEM((n_rows, groups * block), BF16),
                pltpu.VMEM((n_rows, groups * block), BF16),
                pltpu.VMEM((n_rows, 256), F32),
            ],
        ),
        out_shape=[jax.ShapeDtypeStruct((n, width), BF16) for n in parts or (n_rows,)],
        compiler_params=params(),
        cost_estimate=SHORT,
        name="combine",
    )(me, routing, *blocks, *arrived, *wait_for)
    return results if parts else results[0]


def weight_kernel(n_dp, rows, traded_ref, pre_ref, hidden_ref, up_ref, down_ref):
    sums = [None, None]
    for d in range(n_dp):
        for i, factor_ref in enumerate((pre_ref, hidden_ref)):
            part = contract_rows(
                traded_ref[d, i * rows : (i + 1) * rows, :],
                factor_ref[d * rows : (d + 1) * rows, :],
            )
            sums[i] = part if d == 0 else sums[i] + part
    up_ref[0] = sums[0].astype(BF16)
    down_ref[0] = sums[1].astype(BF16)


def weight_grads(traded, pre_all, hidden_all, lanes):
    n_dp, depth, width = traded.shape
    hidden = pre_all.shape[1]
    whole = pl.BlockSpec(pre_all.shape, lambda i: (0, 0))
    return pl.pallas_call(
        functools.partial(weight_kernel, n_dp, depth // 2),
        grid=(width // lanes,),
        in_specs=[pl.BlockSpec((n_dp, depth, lanes), lambda i: (0, 0, i)), whole, whole],
        out_specs=[pl.BlockSpec((1, lanes, hidden), lambda i: (0, i, 0))] * 2,
        out_shape=[jax.ShapeDtypeStruct((1, width, hidden), BF16)] * 2,
        compiler_params=params(),
        cost_estimate=SHORT,
        name="weight_grads",
    )(traded, pre_all, hidden_all)


def after_kernel(*refs):
    pass


def after(values, *others):
    anywhere = pl.BlockSpec(memory_space=pl.ANY)
    return pl.pallas_call(
        after_kernel,
        in_specs=[anywhere] * (1 + len(others)),
        out_specs=anywhere,
        out_shape=jax.ShapeDtypeStruct(values.shape, values.dtype),
        input_output_aliases={0: 0},
        cost_estimate=SHORT,
        name="after",
    )(values, *others)


def permute_xor(values, axis, mask):
    size = lax.axis_size(axis)
    return lax.ppermute(values, axis, [(i, i ^ mask) for i in range(size)])


def exchange(blocks):
    return [blocks[0]] + [permute_xor(blocks[k], "expert", k) for k in range(1, len(blocks))]


def local(tokens, grad_out, expert_ids, gate_codes, w_up, w_down):
    n_expert = lax.axis_size("expert")
    n_dp = lax.axis_size("dp")
    n_rows, width = tokens.shape
    capacity = max(2, 12 * n_rows // (5 * n_expert))
    block = -(-capacity // ROW_TILE) * ROW_TILE
    half = n_expert // 2
    chunk = width // n_dp
    me = lax.axis_index("expert").astype(I32).reshape(1)
    first = jnp.zeros((1,), I32)

    def turned(routing):
        return jnp.pad(routing.T, ((0, 4), (0, 0)))

    def swap_direct(blocks):
        return lax.all_to_all(blocks, "expert", split_axis=0, concat_axis=0, tiled=True)

    routing = jnp.concatenate([expert_ids, gate_codes], axis=1)
    far_routing = permute_xor(routing, "expert", half)
    up_weight = lax.all_gather(w_up, "dp", axis=1, tiled=True)[0]
    down_weight = lax.all_gather(w_down, "dp", axis=1, tiled=True)[0]

    place = (first, turned(routing))
    rows_out = dispatch(*place, tokens, n_expert, block, chunk)
    rows_in = swap_direct(rows_out)
    grads_out = dispatch(*place, grad_out, n_expert, block, chunk, gated=True, wait_for=(rows_out, far_routing))
    grads_in = swap_direct(after(grads_out, rows_in))

    out, sent, hidden, pre_act = forward(me, rows_in, up_weight, down_weight, n_dp)
    parts = (n_rows // 4, n_rows - n_rows // 4)
    far_mixed = combine(
        me, far_routing, exchange(out[half:]), block, chunk, gated=True, parts=parts
    )
    mixed_in = [permute_xor(far_mixed[0], "expert", half)]
    mixed_in.append(permute_xor(after(far_mixed[1], mixed_in[0]), "expert", half))

    near_back, far_back, sent, pre_grad = backward(
        me, grads_in, pre_act, down_weight, up_weight, n_dp, out[:half], sent, far_mixed[0]
    )
    far_back = exchange([after(rows, mixed_in[0]) for rows in far_back])
    far_sum = combine(me, far_routing, far_back, block, chunk, wait_for=(mixed_in[1],))
    sum_in = permute_xor(far_sum, "expert", half)
    near_back = exchange([after(rows, *far_back[1:]) for rows in near_back])
    traded = lax.all_to_all(
        after(sent, mixed_in[0]), "dp", split_axis=0, concat_axis=0, tiled=True
    )
    pre_grad = after(pre_grad, mixed_in[0])
    hidden_all = lax.all_gather(hidden, "dp", axis=0, tiled=True)
    pre_all = lax.all_gather(pre_grad, "dp", axis=0, tiled=True)

    grad_up, grad_down = weight_grads(traded, pre_all, hidden_all, chunk // 5)
    layer_output = combine(
        me,
        routing,
        near_back,
        block,
        chunk,
        gated=True,
        arrived=mixed_in,
        wait_for=(grad_up, grad_down),
    )
    grad_tokens = combine(
        me,
        routing,
        near_back,
        block,
        chunk,
        offset=block,
        arrived=(sum_in,),
        wait_for=(layer_output,),
    )
    return (layer_output, grad_tokens, grad_up, grad_down)


def solution(mesh):
    in_specs = (
        P(("dp", "expert"), None),
        P(("dp", "expert"), None),
        P(("dp", "expert"), None),
        P(("dp", "expert"), None),
        P("expert", "dp", None),
        P("expert", "dp", None),
    )
    out_specs = (
        P(("dp", "expert"), None),
        P(("dp", "expert"), None),
        P("expert", "dp", None),
        P("expert", "dp", None),
    )
    return jax.shard_map(local, mesh=mesh, in_specs=in_specs, out_specs=out_specs, check_vma=False)
```

```python
import functools
import math

import jax
import jax.numpy as jnp
from jax import lax
from jax.experimental import pallas as pl
from jax.experimental.pallas import tpu as pltpu
from jax.sharding import PartitionSpec as P

LAYERS = 40
OUT_SCALE = 1.0 / math.sqrt(2.0 * LAYERS)
ROW_TILE = 8
VMEM_LIMIT = 64 * 1024 * 1024 - 65536
F32, BF16, I32 = jnp.float32, jnp.bfloat16, jnp.int32
GELU_SCALE = math.sqrt(2.0 / math.pi)
GELU_CUBE = 0.044715


def dot(former, latter):
    return jnp.dot(former, latter, preferred_element_type=F32)


def contract_rows(former, latter):
    return lax.dot_general(former, latter, (((0,), (0,)), ((), ())), preferred_element_type=F32)


def contract_columns(former, latter):
    return lax.dot_general(former, latter, (((1,), (1,)), ((), ())), preferred_element_type=F32)


def iota(shape, dim):
    return lax.broadcasted_iota(I32, shape, dim)


def as_bf16(condition):
    return jnp.where(condition, 1.0, 0.0).astype(BF16)


def gelu(v):
    t = jnp.tanh(GELU_SCALE * (v + GELU_CUBE * (v * v * v)))
    return v * (0.5 * (1.0 + t))


def gelu_slope(v):
    t = jnp.tanh(GELU_SCALE * (v + GELU_CUBE * (v * v * v)))
    inner = GELU_SCALE * (1.0 + 3.0 * GELU_CUBE * (v * v))
    return 0.5 * (1.0 + t) + 0.5 * v * (1.0 - t * t) * inner


def stack(pieces):
    return jnp.concatenate([piece.astype(F32) for piece in pieces], axis=0).astype(BF16)


SHORT = pl.CostEstimate(flops=1, bytes_accessed=1, transcendentals=0)


def params(**kwargs):
    return pltpu.CompilerParams(vmem_limit_bytes=VMEM_LIMIT, **kwargs)


def slots_by_row(routing_t, me, half, block):
    n_rows = routing_t.shape[1]
    ids = [routing_t[k : k + 1, :] for k in (0, 1)]
    codes = [routing_t[k : k + 1, :].astype(F32) for k in (2, 3)]
    total = codes[0] + codes[1]
    gates = [code / total for code in codes]
    height = -(-half // 8) * 8
    expert = me ^ iota((height, n_rows), 0)
    named = [ids[k] == expert for k in (0, 1)]
    either = named[0] | named[1]
    earlier = as_bf16(iota((n_rows, n_rows), 0) < iota((n_rows, n_rows), 1))
    before = dot(as_bf16(either), earlier)
    before = jnp.where(either, before, -1.0)
    gate = jnp.where(named[0], gates[0], jnp.where(named[1], gates[1], 0.0))
    place = iota((block, n_rows), 0).astype(F32)
    hot = [jnp.where(place == before[k : k + 1, :], 1.0, 0.0) for k in range(half)]
    slot_gates = [
        jnp.sum(hot[k] * gate[k : k + 1, :], axis=1, keepdims=True) for k in range(half)
    ]
    return jnp.concatenate(hot, axis=0).astype(BF16), jnp.concatenate(slot_gates, axis=0)


def slots_by_column(routing, me, half, block):
    n_rows = routing.shape[0]
    n_slots = half * block
    ids = [routing[:, k : k + 1] for k in (0, 1)]
    codes = [routing[:, k : k + 1].astype(F32) for k in (2, 3)]
    total = codes[0] + codes[1]
    gates = [code / total for code in codes]
    lanes = 128
    expert = me ^ iota((n_rows, lanes), 1)
    within = iota((n_rows, lanes), 1) < half
    either = ((ids[0] == expert) | (ids[1] == expert)) & within
    earlier = as_bf16(iota((n_rows, n_rows), 1) < iota((n_rows, n_rows), 0))
    before = dot(earlier, as_bf16(either))
    slot = iota((lanes, n_slots), 1)
    owner = iota((lanes, n_slots), 0)
    spread = as_bf16((slot >= owner * block) & (slot < (owner + 1) * block))
    before = dot(before.astype(BF16), spread)
    number = dot(as_bf16(iota((n_rows, lanes), 1) >= 0), as_bf16(slot >= (owner + 1) * block))
    slot_row = iota((n_rows, n_slots), 1)
    owner_row = number.astype(I32)
    place = (slot_row - owner_row * block).astype(F32) == before
    slot_expert = me ^ owner_row
    hot = [as_bf16((ids[k] == slot_expert) & place) for k in (0, 1)]
    return hot, gates


def dispatch_kernel(groups, block, gated, n_after, me_ref, routing_ref, *refs):
    source = refs[0]
    out_ref, hot_ref, gate_ref = refs[1 + n_after :]

    @pl.when(pl.program_id(0) == 0)
    def _():
        hot, gate = slots_by_row(routing_ref[...], me_ref[0], groups, block)
        hot_ref[...] = hot
        gate_ref[...] = jnp.broadcast_to(gate, gate_ref.shape)

    rows = dot(hot_ref[...], source[...])
    if gated:
        rows = (OUT_SCALE * gate_ref[:, :1]) * rows
    for k in range(groups):
        out_ref[k] = rows[k * block : (k + 1) * block].astype(BF16)


def dispatch(me, routing_t, source, groups, block, chunk, gated=False, wait_for=()):
    n_rows, width = source.shape
    return pl.pallas_call(
        functools.partial(dispatch_kernel, groups, block, gated, len(wait_for)),
        grid_spec=pltpu.PrefetchScalarGridSpec(
            num_scalar_prefetch=1,
            grid=(width // chunk,),
            in_specs=[
                pl.BlockSpec(routing_t.shape, lambda d, me: (0, 0)),
                pl.BlockSpec((n_rows, chunk), lambda d, me: (0, d)),
            ]
            + [pl.BlockSpec(memory_space=pl.ANY) for _ in wait_for],
            out_specs=pl.BlockSpec((groups, block, chunk), lambda d, me: (0, 0, d)),
            scratch_shapes=[
                pltpu.VMEM((groups * block, n_rows), BF16),
                pltpu.VMEM((groups * block, 128), F32),
            ],
        ),
        out_shape=jax.ShapeDtypeStruct((groups, block, width), BF16),
        compiler_params=params(),
        cost_estimate=SHORT,
        name="dispatch",
    )(me, routing_t, source, *wait_for)


def expert_kernel(n, n_chunks, backward, *refs):
    me_ref, rows_hbm, first_hbm, second_hbm = refs[:4]
    at = 7 if backward else 4
    outs = refs[at : at + n]
    sent_hbm, middle_ref = refs[at + n : at + n + 2]
    pre_ref = refs[4] if backward else refs[at + n + 2]
    rows_v, first_v, second_v, out_v, in_sem, out_sem = refs[-6:]
    rows, width = rows_v.shape
    chunk = width // n_chunks
    columns = [pl.ds(d * chunk, chunk) for d in range(n_chunks)]

    def load(d):
        return [
            pltpu.make_async_copy(
                rows_hbm.at[:, columns[d]], rows_v.at[:, columns[d]], in_sem.at[0, d]
            ),
            pltpu.make_async_copy(first_hbm.at[columns[d]], first_v.at[columns[d]], in_sem.at[1, d]),
        ]

    def load_second(d):
        return pltpu.make_async_copy(
            second_hbm.at[columns[d]], second_v.at[columns[d]], in_sem.at[2, d]
        )

    def send(d):
        target = sent_hbm.at[d, pl.ds(rows if backward else 0, rows)]
        return pltpu.make_async_copy(rows_v.at[:, columns[d]], target, in_sem.at[3, d])

    def store(d, k):
        return pltpu.make_async_copy(
            out_v.at[me_ref[0] ^ k, :, columns[d]], outs[k].at[:, columns[d]], out_sem.at[d, k]
        )

    for d in range(n_chunks):
        for copy in load(d):
            copy.start()
    for d in range(n_chunks):
        load_second(d).start()
    total = None
    for d in range(n_chunks):
        for copy in load(d):
            copy.wait()
        send(d).start()
        part = dot(rows_v[:, columns[d]], first_v[columns[d]])
        total = part if d == 0 else total + part
    if backward:
        middle = (total * gelu_slope(pre_ref[...])).astype(BF16)
    else:
        pre_ref[...] = total
        middle = gelu(total).astype(BF16)
    middle_ref[...] = middle
    for d in range(n_chunks):
        load_second(d).wait()
        result = contract_columns(middle, second_v[columns[d]])
        out_v[:, :, columns[d]] = result.reshape(n, rows // n, chunk).astype(BF16)
        for k in range(n):
            store(d, k).start()
    for d in range(n_chunks):
        send(d).wait()
        for k in range(n):
            store(d, k).wait()


def expert(me, rows_in, first, second, n_chunks, pre=None, sent=None, wait_for=None):
    n, block, width = rows_in.shape
    rows = n * block
    hidden = first.shape[1]
    chunk = width // n_chunks
    backward = pre is not None
    anywhere = pl.BlockSpec(memory_space=pl.ANY)
    whole = pl.BlockSpec(memory_space=pltpu.VMEM)
    operands = (me, rows_in.reshape(rows, width), first, second)
    in_specs = [pl.BlockSpec(memory_space=pltpu.SMEM)] + [anywhere] * 3
    if backward:
        operands += (pre, sent, wait_for)
        in_specs += [whole, anywhere, anywhere]
    results = pl.pallas_call(
        functools.partial(expert_kernel, n, n_chunks, backward),
        in_specs=in_specs,
        out_specs=[anywhere] * (n + 1) + [whole] * (1 if backward else 2),
        out_shape=[jax.ShapeDtypeStruct((block, width), BF16)] * n
        + [
            jax.ShapeDtypeStruct((n_chunks, 2 * rows, chunk), BF16),
            jax.ShapeDtypeStruct((rows, hidden), BF16),
        ]
        + ([] if backward else [jax.ShapeDtypeStruct((rows, hidden), F32)]),
        scratch_shapes=[
            pltpu.VMEM((rows, width), BF16),
            pltpu.VMEM((width, hidden), BF16),
            pltpu.VMEM((width, hidden), BF16),
            pltpu.VMEM((n, block, width), BF16),
            pltpu.SemaphoreType.DMA((4, n_chunks)),
            pltpu.SemaphoreType.DMA((n_chunks, n)),
        ],
        input_output_aliases={5: n} if backward else {},
        compiler_params=params(),
        cost_estimate=SHORT,
        name="expert_backward" if backward else "expert_forward",
    )(*operands)
    return (results[:n],) + tuple(results[n:])


def combine_kernel(groups, block, gated, n_arrived, n_after, me_ref, routing_ref, *refs):
    n_blocks = groups
    blocks = refs[:n_blocks]
    arrived = refs[n_blocks : n_blocks + n_arrived]
    outs = refs[n_blocks + n_arrived + n_after : -2]
    hot_ref, gate_ref = refs[-2:]

    @pl.when(pl.program_id(0) == 0)
    def _():
        hot, gates = slots_by_column(routing_ref[...], me_ref[0], groups, block)
        if gated:
            hot_ref[...] = jnp.concatenate(hot, axis=0)
            for k in (0, 1):
                gate_ref[:, k * 128 : (k + 1) * 128] = jnp.broadcast_to(
                    OUT_SCALE * gates[k], (gates[k].shape[0], 128)
                )
        else:
            hot_ref[...] = (hot[0].astype(F32) + hot[1].astype(F32)).astype(BF16)

    rows = stack([ref[...] for ref in blocks])
    n_rows = routing_ref.shape[0]
    total = dot(hot_ref[...], rows)
    if gated:
        total = gate_ref[:, :1] * total[:n_rows] + gate_ref[:, 128:129] * total[n_rows:]
    if arrived:
        total = total + jnp.concatenate([ref[...].astype(F32) for ref in arrived], axis=0)
    at = 0
    for ref in outs:
        ref[...] = total[at : at + ref.shape[0]].astype(BF16)
        at += ref.shape[0]


def combine(
    me, routing, blocks, block, chunk, gated=False, arrived=(), wait_for=(), parts=None
):
    n_rows = routing.shape[0]
    groups = len(blocks)
    width = blocks[0].shape[1]
    by_rows = lambda n: pl.BlockSpec((n, chunk), lambda d, me: (0, d))
    results = pl.pallas_call(
        functools.partial(
            combine_kernel, groups, block, gated, len(arrived), len(wait_for)
        ),
        grid_spec=pltpu.PrefetchScalarGridSpec(
            num_scalar_prefetch=1,
            grid=(width // chunk,),
            in_specs=[pl.BlockSpec(routing.shape, lambda d, me: (0, 0))]
            + [by_rows(block) for _ in blocks]
            + [by_rows(rows.shape[0]) for rows in arrived]
            + [pl.BlockSpec(memory_space=pl.ANY) for _ in wait_for],
            out_specs=[by_rows(n) for n in parts or (n_rows,)],
            scratch_shapes=[
                pltpu.VMEM(((2 if gated else 1) * n_rows, groups * block), BF16),
                pltpu.VMEM((n_rows, 256), F32),
            ],
        ),
        out_shape=[jax.ShapeDtypeStruct((n, width), BF16) for n in parts or (n_rows,)],
        compiler_params=params(),
        cost_estimate=SHORT,
        name="combine",
    )(me, routing, *blocks, *arrived, *wait_for)
    return results if parts else results[0]


def weight_kernel(n_dp, rows, traded_ref, pre_ref, hidden_ref, *outs):
    for i, factor_ref in enumerate((pre_ref, hidden_ref)):
        total = None
        for d in range(n_dp):
            part = contract_rows(
                traded_ref[d, i * rows : (i + 1) * rows, :],
                factor_ref[d * rows : (d + 1) * rows, :],
            )
            total = part if d == 0 else total + part
        outs[i][0] = total.astype(BF16)


def weight_grads(traded, pre_all, hidden_all, lanes):
    n_dp, depth, width = traded.shape
    hidden = pre_all.shape[1]
    whole = pl.BlockSpec(pre_all.shape, lambda i: (0, 0))
    return pl.pallas_call(
        functools.partial(weight_kernel, n_dp, depth // 2),
        grid=(width // lanes,),
        in_specs=[pl.BlockSpec((n_dp, depth, lanes), lambda i: (0, 0, i)), whole, whole],
        out_specs=[pl.BlockSpec((1, lanes, hidden), lambda i: (0, i, 0))] * 2,
        out_shape=[jax.ShapeDtypeStruct((1, width, hidden), BF16)] * 2,
        compiler_params=params(),
        cost_estimate=SHORT,
        name="weight_grads",
    )(traded, pre_all, hidden_all)


def after_kernel(*refs):
    pass


def after(values, *others):
    anywhere = pl.BlockSpec(memory_space=pl.ANY)
    return pl.pallas_call(
        after_kernel,
        in_specs=[anywhere] * (1 + len(others)),
        out_specs=anywhere,
        out_shape=jax.ShapeDtypeStruct(values.shape, values.dtype),
        input_output_aliases={0: 0},
        cost_estimate=SHORT,
        name="after",
    )(values, *others)


def permute_xor(values, axis, mask):
    size = lax.axis_size(axis)
    return lax.ppermute(values, axis, [(i, i ^ mask) for i in range(size)])


def exchange(blocks):
    return [blocks[0]] + [permute_xor(blocks[k], "expert", k) for k in range(1, len(blocks))]


def local(tokens, grad_out, expert_ids, gate_codes, w_up, w_down):
    n_expert = lax.axis_size("expert")
    n_dp = lax.axis_size("dp")
    n_rows, width = tokens.shape
    capacity = max(2, 12 * n_rows // (5 * n_expert))
    block = -(-capacity // ROW_TILE) * ROW_TILE
    half = n_expert // 2
    chunk = width // 2
    me = lax.axis_index("expert").astype(I32).reshape(1)
    first = jnp.zeros((1,), I32)

    def turned(routing):
        return jnp.pad(routing.T, ((0, 4), (0, 0)))

    def swap_direct(blocks):
        return lax.all_to_all(blocks, "expert", split_axis=0, concat_axis=0, tiled=True)

    routing = jnp.concatenate([expert_ids, gate_codes], axis=1)
    far_routing = permute_xor(routing, "expert", half)
    up_weight = lax.all_gather(w_up, "dp", axis=1, tiled=True)[0]
    down_weight = lax.all_gather(w_down, "dp", axis=1, tiled=True)[0]

    place = (first, turned(routing))
    rows_out = dispatch(*place, tokens, n_expert, block, chunk)
    rows_in = swap_direct(rows_out)
    grads_out = dispatch(*place, grad_out, n_expert, block, chunk, gated=True, wait_for=(rows_out,))
    grads_in = swap_direct(after(grads_out, far_routing))

    out, sent, hidden, pre_act = expert(me, rows_in, up_weight, down_weight, n_dp)
    parts = (n_rows // 4, n_rows - n_rows // 4)
    far_mixed = combine(
        me, far_routing, exchange(out[half:]), block, chunk, gated=True, parts=parts
    )
    mixed_in = [permute_xor(far_mixed[0], "expert", half)]
    mixed_in.append(permute_xor(after(far_mixed[1], mixed_in[0]), "expert", half))

    row_grads, sent, pre_grad = expert(
        me, grads_in, down_weight, up_weight, n_dp, pre=pre_act, sent=sent, wait_for=far_mixed[0]
    )
    far_back = exchange([after(rows, mixed_in[0]) for rows in row_grads[half:]])
    far_sum = combine(me, far_routing, far_back, block, chunk, wait_for=(mixed_in[1],))
    sum_in = permute_xor(far_sum, "expert", half)
    near_back = exchange([after(rows, *far_back[1:]) for rows in out[:half]])
    near_grad = exchange([after(rows, far_sum) for rows in row_grads[:half]])
    traded = lax.all_to_all(
        after(sent, mixed_in[0]), "dp", split_axis=0, concat_axis=0, tiled=True
    )
    hidden_all = lax.all_gather(hidden, "dp", axis=0, tiled=True)
    pre_all = lax.all_gather(after(pre_grad, mixed_in[0]), "dp", axis=0, tiled=True)

    grad_up, grad_down = weight_grads(traded, pre_all, hidden_all, 256)
    layer_output = combine(
        me,
        routing,
        near_back,
        block,
        chunk,
        gated=True,
        arrived=mixed_in,
        wait_for=(grad_up, grad_down),
    )
    grad_tokens = combine(
        me, routing, near_grad, block, chunk, arrived=(sum_in,), wait_for=(layer_output,)
    )
    return (layer_output, grad_tokens, grad_up, grad_down)


def solution(mesh):
    in_specs = (
        P(("dp", "expert"), None),
        P(("dp", "expert"), None),
        P(("dp", "expert"), None),
        P(("dp", "expert"), None),
        P("expert", "dp", None),
        P("expert", "dp", None),
    )
    out_specs = (
        P(("dp", "expert"), None),
        P(("dp", "expert"), None),
        P("expert", "dp", None),
        P("expert", "dp", None),
    )
    return jax.shard_map(local, mesh=mesh, in_specs=in_specs, out_specs=out_specs, check_vma=False)
```

```python
import functools
import math

import jax
import jax.numpy as jnp
from jax import lax
from jax.experimental import pallas as pl
from jax.experimental.pallas import tpu as pltpu
from jax.sharding import PartitionSpec as P

LAYERS = 40
OUT_SCALE = 1.0 / math.sqrt(2.0 * LAYERS)
ROW_TILE = 8
VMEM_LIMIT = 64 * 1024 * 1024 - 65536
F32, BF16, I32 = jnp.float32, jnp.bfloat16, jnp.int32
GELU_SCALE = math.sqrt(2.0 / math.pi)
GELU_CUBE = 0.044715


def dot(former, latter):
    return jnp.dot(former, latter, preferred_element_type=F32)


def contract_rows(former, latter):
    return lax.dot_general(former, latter, (((0,), (0,)), ((), ())), preferred_element_type=F32)


def contract_columns(former, latter):
    return lax.dot_general(former, latter, (((1,), (1,)), ((), ())), preferred_element_type=F32)


def iota(shape, dim):
    return lax.broadcasted_iota(I32, shape, dim)


def as_bf16(condition):
    return jnp.where(condition, 1.0, 0.0).astype(BF16)


def gelu(v):
    t = jnp.tanh(GELU_SCALE * (v + GELU_CUBE * (v * v * v)))
    return v * (0.5 * (1.0 + t))


def gelu_slope(v):
    t = jnp.tanh(GELU_SCALE * (v + GELU_CUBE * (v * v * v)))
    inner = GELU_SCALE * (1.0 + 3.0 * GELU_CUBE * (v * v))
    return 0.5 * (1.0 + t) + 0.5 * v * (1.0 - t * t) * inner


def stack(pieces):
    return jnp.concatenate([piece.astype(F32) for piece in pieces], axis=0).astype(BF16)


SHORT = pl.CostEstimate(flops=1, bytes_accessed=1, transcendentals=0)


def params(**kwargs):
    return pltpu.CompilerParams(vmem_limit_bytes=VMEM_LIMIT, **kwargs)


def slots_by_row(routing_t, me, half, block):
    n_rows = routing_t.shape[1]
    ids = [routing_t[k : k + 1, :] for k in (0, 1)]
    codes = [routing_t[k : k + 1, :].astype(F32) for k in (2, 3)]
    total = codes[0] + codes[1]
    gates = [code / total for code in codes]
    height = -(-half // 8) * 8
    expert = me ^ iota((height, n_rows), 0)
    named = [ids[k] == expert for k in (0, 1)]
    either = named[0] | named[1]
    earlier = as_bf16(iota((n_rows, n_rows), 0) < iota((n_rows, n_rows), 1))
    before = dot(as_bf16(either), earlier)
    before = jnp.where(either, before, -1.0)
    gate = jnp.where(named[0], gates[0], jnp.where(named[1], gates[1], 0.0))
    place = iota((block, n_rows), 0).astype(F32)
    hot = [jnp.where(place == before[k : k + 1, :], 1.0, 0.0) for k in range(half)]
    slot_gates = [
        jnp.sum(hot[k] * gate[k : k + 1, :], axis=1, keepdims=True) for k in range(half)
    ]
    return jnp.concatenate(hot, axis=0).astype(BF16), jnp.concatenate(slot_gates, axis=0)


def slots_by_column(routing, me, half, block):
    n_rows = routing.shape[0]
    n_slots = half * block
    ids = [routing[:, k : k + 1] for k in (0, 1)]
    codes = [routing[:, k : k + 1].astype(F32) for k in (2, 3)]
    total = codes[0] + codes[1]
    gates = [code / total for code in codes]
    lanes = 128
    expert = me ^ iota((n_rows, lanes), 1)
    within = iota((n_rows, lanes), 1) < half
    either = ((ids[0] == expert) | (ids[1] == expert)) & within
    earlier = as_bf16(iota((n_rows, n_rows), 1) < iota((n_rows, n_rows), 0))
    before = dot(earlier, as_bf16(either))
    slot = iota((lanes, n_slots), 1)
    owner = iota((lanes, n_slots), 0)
    spread = as_bf16((slot >= owner * block) & (slot < (owner + 1) * block))
    before = dot(before.astype(BF16), spread)
    number = dot(as_bf16(iota((n_rows, lanes), 1) >= 0), as_bf16(slot >= (owner + 1) * block))
    slot_row = iota((n_rows, n_slots), 1)
    owner_row = number.astype(I32)
    place = (slot_row - owner_row * block).astype(F32) == before
    slot_expert = me ^ owner_row
    hot = [as_bf16((ids[k] == slot_expert) & place) for k in (0, 1)]
    return hot, gates


def dispatch_kernel(groups, block, gated, n_after, me_ref, routing_ref, *refs):
    source = refs[0]
    out_ref, hot_ref, gate_ref = refs[1 + n_after :]

    @pl.when(pl.program_id(0) == 0)
    def _():
        hot, gate = slots_by_row(routing_ref[...], me_ref[0], groups, block)
        hot_ref[...] = hot
        gate_ref[...] = jnp.broadcast_to(gate, gate_ref.shape)

    rows = dot(hot_ref[...], source[...])
    if gated:
        rows = (OUT_SCALE * gate_ref[:, :1]) * rows
    for k in range(groups):
        out_ref[k] = rows[k * block : (k + 1) * block].astype(BF16)


def dispatch(me, routing_t, source, groups, block, chunk, gated=False, wait_for=()):
    n_rows, width = source.shape
    return pl.pallas_call(
        functools.partial(dispatch_kernel, groups, block, gated, len(wait_for)),
        grid_spec=pltpu.PrefetchScalarGridSpec(
            num_scalar_prefetch=1,
            grid=(width // chunk,),
            in_specs=[
                pl.BlockSpec(routing_t.shape, lambda d, me: (0, 0)),
                pl.BlockSpec((n_rows, chunk), lambda d, me: (0, d)),
            ]
            + [pl.BlockSpec(memory_space=pl.ANY) for _ in wait_for],
            out_specs=pl.BlockSpec((groups, block, chunk), lambda d, me: (0, 0, d)),
            scratch_shapes=[
                pltpu.VMEM((groups * block, n_rows), BF16),
                pltpu.VMEM((groups * block, 128), F32),
            ],
        ),
        out_shape=jax.ShapeDtypeStruct((groups, block, width), BF16),
        compiler_params=params(),
        cost_estimate=SHORT,
        name="dispatch",
    )(me, routing_t, source, *wait_for)


def expert_kernel(n, n_chunks, backward, *refs):
    me_ref, rows_hbm, first_hbm, second_hbm = refs[:4]
    at = 7 if backward else 4
    outs = refs[at : at + n]
    sent_hbm, middle_ref = refs[at + n : at + n + 2]
    pre_ref = refs[4] if backward else refs[at + n + 2]
    rows_v, first_v, second_v, out_v, in_sem, out_sem = refs[-6:]
    rows, width = rows_v.shape
    chunk = width // n_chunks
    columns = [pl.ds(d * chunk, chunk) for d in range(n_chunks)]

    def load(d):
        return [
            pltpu.make_async_copy(
                rows_hbm.at[:, columns[d]], rows_v.at[:, columns[d]], in_sem.at[0, d]
            ),
            pltpu.make_async_copy(first_hbm.at[columns[d]], first_v.at[columns[d]], in_sem.at[1, d]),
        ]

    def load_second(d):
        return pltpu.make_async_copy(
            second_hbm.at[columns[d]], second_v.at[columns[d]], in_sem.at[2, d]
        )

    def send(d):
        target = sent_hbm.at[d, pl.ds(rows if backward else 0, rows)]
        return pltpu.make_async_copy(rows_v.at[:, columns[d]], target, in_sem.at[3, d])

    def store(d, k):
        return pltpu.make_async_copy(
            out_v.at[me_ref[0] ^ k, :, columns[d]], outs[k].at[:, columns[d]], out_sem.at[d, k]
        )

    for d in range(n_chunks):
        for copy in load(d):
            copy.start()
    for d in range(n_chunks):
        load_second(d).start()
    total = None
    for d in range(n_chunks):
        for copy in load(d):
            copy.wait()
        send(d).start()
        part = dot(rows_v[:, columns[d]], first_v[columns[d]])
        total = part if d == 0 else total + part
    if backward:
        middle = (total * gelu_slope(pre_ref[...])).astype(BF16)
    else:
        pre_ref[...] = total
        middle = gelu(total).astype(BF16)
    middle_ref[...] = middle
    for d in range(n_chunks):
        load_second(d).wait()
        result = contract_columns(middle, second_v[columns[d]])
        out_v[:, :, columns[d]] = result.reshape(n, rows // n, chunk).astype(BF16)
        for k in range(n):
            store(d, k).start()
    for d in range(n_chunks):
        send(d).wait()
        for k in range(n):
            store(d, k).wait()


def expert(me, rows_in, first, second, n_chunks, pre=None, sent=None, wait_for=None):
    n, block, width = rows_in.shape
    rows = n * block
    hidden = first.shape[1]
    chunk = width // n_chunks
    backward = pre is not None
    anywhere = pl.BlockSpec(memory_space=pl.ANY)
    whole = pl.BlockSpec(memory_space=pltpu.VMEM)
    operands = (me, rows_in.reshape(rows, width), first, second)
    in_specs = [pl.BlockSpec(memory_space=pltpu.SMEM)] + [anywhere] * 3
    if backward:
        operands += (pre, sent, wait_for)
        in_specs += [whole, anywhere, anywhere]
    results = pl.pallas_call(
        functools.partial(expert_kernel, n, n_chunks, backward),
        in_specs=in_specs,
        out_specs=[anywhere] * (n + 1) + [whole] * (1 if backward else 2),
        out_shape=[jax.ShapeDtypeStruct((block, width), BF16)] * n
        + [
            jax.ShapeDtypeStruct((n_chunks, 2 * rows, chunk), BF16),
            jax.ShapeDtypeStruct((rows, hidden), BF16),
        ]
        + ([] if backward else [jax.ShapeDtypeStruct((rows, hidden), F32)]),
        scratch_shapes=[
            pltpu.VMEM((rows, width), BF16),
            pltpu.VMEM((width, hidden), BF16),
            pltpu.VMEM((width, hidden), BF16),
            pltpu.VMEM((n, block, width), BF16),
            pltpu.SemaphoreType.DMA((4, n_chunks)),
            pltpu.SemaphoreType.DMA((n_chunks, n)),
        ],
        input_output_aliases={5: n} if backward else {},
        compiler_params=params(),
        cost_estimate=SHORT,
        name="expert_backward" if backward else "expert_forward",
    )(*operands)
    return (results[:n],) + tuple(results[n:])


def combine_kernel(groups, block, gated, n_arrived, n_after, me_ref, routing_ref, *refs):
    n_blocks = groups
    blocks = refs[:n_blocks]
    arrived = refs[n_blocks : n_blocks + n_arrived]
    outs = refs[n_blocks + n_arrived + n_after : -2]
    hot_ref, gate_ref = refs[-2:]

    @pl.when(pl.program_id(0) == 0)
    def _():
        hot, gates = slots_by_column(routing_ref[...], me_ref[0], groups, block)
        if gated:
            hot_ref[...] = jnp.concatenate(hot, axis=0)
            for k in (0, 1):
                gate_ref[:, k * 128 : (k + 1) * 128] = jnp.broadcast_to(
                    OUT_SCALE * gates[k], (gates[k].shape[0], 128)
                )
        else:
            hot_ref[...] = (hot[0].astype(F32) + hot[1].astype(F32)).astype(BF16)

    rows = stack([ref[...] for ref in blocks])
    n_rows = routing_ref.shape[0]
    total = dot(hot_ref[...], rows)
    if gated:
        total = gate_ref[:, :1] * total[:n_rows] + gate_ref[:, 128:129] * total[n_rows:]
    if arrived:
        total = total + jnp.concatenate([ref[...].astype(F32) for ref in arrived], axis=0)
    at = 0
    for ref in outs:
        ref[...] = total[at : at + ref.shape[0]].astype(BF16)
        at += ref.shape[0]


def combine(
    me, routing, blocks, block, chunk, gated=False, arrived=(), wait_for=(), parts=None
):
    n_rows = routing.shape[0]
    groups = len(blocks)
    width = blocks[0].shape[1]
    by_rows = lambda n: pl.BlockSpec((n, chunk), lambda d, me: (0, d))
    results = pl.pallas_call(
        functools.partial(
            combine_kernel, groups, block, gated, len(arrived), len(wait_for)
        ),
        grid_spec=pltpu.PrefetchScalarGridSpec(
            num_scalar_prefetch=1,
            grid=(width // chunk,),
            in_specs=[pl.BlockSpec(routing.shape, lambda d, me: (0, 0))]
            + [by_rows(block) for _ in blocks]
            + [by_rows(rows.shape[0]) for rows in arrived]
            + [pl.BlockSpec(memory_space=pl.ANY) for _ in wait_for],
            out_specs=[by_rows(n) for n in parts or (n_rows,)],
            scratch_shapes=[
                pltpu.VMEM(((2 if gated else 1) * n_rows, groups * block), BF16),
                pltpu.VMEM((n_rows, 256), F32),
            ],
        ),
        out_shape=[jax.ShapeDtypeStruct((n, width), BF16) for n in parts or (n_rows,)],
        compiler_params=params(),
        cost_estimate=SHORT,
        name="combine",
    )(me, routing, *blocks, *arrived, *wait_for)
    return results if parts else results[0]


def weight_kernel(n_dp, rows, traded_ref, pre_ref, hidden_ref, *outs):
    for i, factor_ref in enumerate((pre_ref, hidden_ref)):
        total = None
        for d in range(n_dp):
            part = contract_rows(
                traded_ref[d, i * rows : (i + 1) * rows, :],
                factor_ref[d * rows : (d + 1) * rows, :],
            )
            total = part if d == 0 else total + part
        outs[i][0] = total.astype(BF16)


def weight_grads(traded, pre_all, hidden_all, lanes):
    n_dp, depth, width = traded.shape
    hidden = pre_all.shape[1]
    whole = pl.BlockSpec(pre_all.shape, lambda i: (0, 0))
    return pl.pallas_call(
        functools.partial(weight_kernel, n_dp, depth // 2),
        grid=(width // lanes,),
        in_specs=[pl.BlockSpec((n_dp, depth, lanes), lambda i: (0, 0, i)), whole, whole],
        out_specs=[pl.BlockSpec((1, lanes, hidden), lambda i: (0, i, 0))] * 2,
        out_shape=[jax.ShapeDtypeStruct((1, width, hidden), BF16)] * 2,
        compiler_params=params(),
        cost_estimate=SHORT,
        name="weight_grads",
    )(traded, pre_all, hidden_all)


def after_kernel(*refs):
    pass


def after(values, *others):
    anywhere = pl.BlockSpec(memory_space=pl.ANY)
    return pl.pallas_call(
        after_kernel,
        in_specs=[anywhere] * (1 + len(others)),
        out_specs=anywhere,
        out_shape=jax.ShapeDtypeStruct(values.shape, values.dtype),
        input_output_aliases={0: 0},
        cost_estimate=SHORT,
        name="after",
    )(values, *others)


def permute_xor(values, axis, mask):
    size = lax.axis_size(axis)
    return lax.ppermute(values, axis, [(i, i ^ mask) for i in range(size)])


def exchange(blocks):
    return [blocks[0]] + [permute_xor(blocks[k], "expert", k) for k in range(1, len(blocks))]


def local(tokens, grad_out, expert_ids, gate_codes, w_up, w_down):
    n_expert = lax.axis_size("expert")
    n_dp = lax.axis_size("dp")
    n_rows, width = tokens.shape
    capacity = max(2, 12 * n_rows // (5 * n_expert))
    block = -(-capacity // ROW_TILE) * ROW_TILE
    half = n_expert // 2
    chunk = width // 2
    me = lax.axis_index("expert").astype(I32).reshape(1)
    first = jnp.zeros((1,), I32)

    def turned(routing):
        return jnp.pad(routing.T, ((0, 4), (0, 0)))

    def swap_direct(blocks):
        return lax.all_to_all(blocks, "expert", split_axis=0, concat_axis=0, tiled=True)

    routing = jnp.concatenate([expert_ids, gate_codes], axis=1)
    far_routing = permute_xor(routing, "expert", half)
    up_weight = lax.all_gather(w_up, "dp", axis=1, tiled=True)[0]
    down_weight = lax.all_gather(w_down, "dp", axis=1, tiled=True)[0]

    place = (first, turned(routing))
    rows_out = dispatch(*place, tokens, n_expert, block, chunk)
    rows_in = swap_direct(rows_out)
    grads_out = dispatch(*place, grad_out, n_expert, block, chunk, gated=True, wait_for=(rows_out,))
    grads_in = swap_direct(after(grads_out, far_routing))

    out, sent, hidden, pre_act = expert(me, rows_in, up_weight, down_weight, n_dp)
    parts = (n_rows // 4, n_rows - n_rows // 4)
    far_out = exchange(out[half:])
    far_mixed = combine(me, far_routing, far_out, block, chunk, gated=True, parts=parts)
    near_back = exchange([after(rows, far_out[1]) for rows in out[:half]])
    mixed_in = [permute_xor(far_mixed[0], "expert", half)]
    mixed_in.append(permute_xor(after(far_mixed[1], mixed_in[0]), "expert", half))

    row_grads, sent, pre_grad = expert(
        me, grads_in, down_weight, up_weight, n_dp, pre=pre_act, sent=sent, wait_for=far_mixed[0]
    )
    ready = (mixed_in[0], *near_back[1:])
    far_back = exchange([after(rows, *ready) for rows in row_grads[half:]])
    far_sum = combine(me, far_routing, far_back, block, chunk, wait_for=(mixed_in[1],))
    sum_in = permute_xor(far_sum, "expert", half)
    near_grad = exchange([after(rows, far_sum) for rows in row_grads[:half]])
    traded = lax.all_to_all(
        after(sent, *ready), "dp", split_axis=0, concat_axis=0, tiled=True
    )
    hidden_all = lax.all_gather(hidden, "dp", axis=0, tiled=True)
    pre_all = lax.all_gather(after(pre_grad, *ready), "dp", axis=0, tiled=True)

    grad_up, grad_down = weight_grads(traded, pre_all, hidden_all, 256)
    layer_output = combine(
        me,
        routing,
        near_back,
        block,
        chunk,
        gated=True,
        arrived=mixed_in,
        wait_for=(grad_up, grad_down),
    )
    grad_tokens = combine(
        me, routing, near_grad, block, chunk, arrived=(sum_in,), wait_for=(layer_output,)
    )
    return (layer_output, grad_tokens, grad_up, grad_down)


def solution(mesh):
    in_specs = (
        P(("dp", "expert"), None),
        P(("dp", "expert"), None),
        P(("dp", "expert"), None),
        P(("dp", "expert"), None),
        P("expert", "dp", None),
        P("expert", "dp", None),
    )
    out_specs = (
        P(("dp", "expert"), None),
        P(("dp", "expert"), None),
        P("expert", "dp", None),
        P("expert", "dp", None),
    )
    return jax.shard_map(local, mesh=mesh, in_specs=in_specs, out_specs=out_specs, check_vma=False)
```

```python
import functools
import math

import jax
import jax.numpy as jnp
from jax import lax
from jax.experimental import pallas as pl
from jax.experimental.pallas import tpu as pltpu
from jax.sharding import PartitionSpec as P

LAYERS = 40
OUT_SCALE = 1.0 / math.sqrt(2.0 * LAYERS)
ROW_TILE = 8
VMEM_LIMIT = 64 * 1024 * 1024 - 65536
F32, BF16, I32 = jnp.float32, jnp.bfloat16, jnp.int32
GELU_SCALE = math.sqrt(2.0 / math.pi)
GELU_CUBE = 0.044715


def dot(former, latter):
    return jnp.dot(former, latter, preferred_element_type=F32)


def contract_rows(former, latter):
    return lax.dot_general(former, latter, (((0,), (0,)), ((), ())), preferred_element_type=F32)


def contract_columns(former, latter):
    return lax.dot_general(former, latter, (((1,), (1,)), ((), ())), preferred_element_type=F32)


def iota(shape, dim):
    return lax.broadcasted_iota(I32, shape, dim)


def as_bf16(condition):
    return jnp.where(condition, 1.0, 0.0).astype(BF16)


def gelu(v):
    t = jnp.tanh(GELU_SCALE * (v + GELU_CUBE * (v * v * v)))
    return v * (0.5 * (1.0 + t))


def gelu_slope(v):
    t = jnp.tanh(GELU_SCALE * (v + GELU_CUBE * (v * v * v)))
    inner = GELU_SCALE * (1.0 + 3.0 * GELU_CUBE * (v * v))
    return 0.5 * (1.0 + t) + 0.5 * v * (1.0 - t * t) * inner


def stack(pieces):
    return jnp.concatenate([piece.astype(F32) for piece in pieces], axis=0).astype(BF16)


SHORT = pl.CostEstimate(flops=1, bytes_accessed=1, transcendentals=0)


def params(**kwargs):
    return pltpu.CompilerParams(vmem_limit_bytes=VMEM_LIMIT, **kwargs)


def slots_by_row(routing, half, block):
    n_rows = routing.shape[0]
    lane = iota((n_rows, 128), 1)
    wide = jnp.zeros((n_rows, 128), F32)
    for k in range(4):
        wide = jnp.where(lane == k, routing[:, k : k + 1].astype(F32), wide)
    turned = wide.T
    ids = [turned[k : k + 1, :].astype(I32) for k in (0, 1)]
    codes = [turned[k : k + 1, :] for k in (2, 3)]
    total = codes[0] + codes[1]
    gates = [code / total for code in codes]
    height = -(-half // 8) * 8
    expert = iota((height, n_rows), 0)
    named = [ids[k] == expert for k in (0, 1)]
    either = named[0] | named[1]
    earlier = as_bf16(iota((n_rows, n_rows), 0) < iota((n_rows, n_rows), 1))
    before = dot(as_bf16(either), earlier)
    before = jnp.where(either, before, -1.0)
    gate = jnp.where(named[0], gates[0], jnp.where(named[1], gates[1], 0.0))
    place = iota((block, n_rows), 0).astype(F32)
    hot = [jnp.where(place == before[k : k + 1, :], 1.0, 0.0) for k in range(half)]
    slot_gates = [
        jnp.sum(hot[k] * gate[k : k + 1, :], axis=1, keepdims=True) for k in range(half)
    ]
    return jnp.concatenate(hot, axis=0).astype(BF16), jnp.concatenate(slot_gates, axis=0)


def slots_by_column(routing, me, half, block):
    n_rows = routing.shape[0]
    n_slots = half * block
    ids = [routing[:, k : k + 1] for k in (0, 1)]
    codes = [routing[:, k : k + 1].astype(F32) for k in (2, 3)]
    total = codes[0] + codes[1]
    gates = [code / total for code in codes]
    lanes = 128
    expert = me ^ iota((n_rows, lanes), 1)
    within = iota((n_rows, lanes), 1) < half
    either = ((ids[0] == expert) | (ids[1] == expert)) & within
    earlier = as_bf16(iota((n_rows, n_rows), 1) < iota((n_rows, n_rows), 0))
    before = dot(earlier, as_bf16(either))
    slot = iota((lanes, n_slots), 1)
    owner = iota((lanes, n_slots), 0)
    spread = as_bf16((slot >= owner * block) & (slot < (owner + 1) * block))
    before = dot(before.astype(BF16), spread)
    number = dot(as_bf16(iota((n_rows, lanes), 1) >= 0), as_bf16(slot >= (owner + 1) * block))
    slot_row = iota((n_rows, n_slots), 1)
    owner_row = number.astype(I32)
    place = (slot_row - owner_row * block).astype(F32) == before
    slot_expert = me ^ owner_row
    hot = [as_bf16((ids[k] == slot_expert) & place) for k in (0, 1)]
    return hot, gates


def dispatch_kernel(groups, block, gated, n_after, routing_ref, *refs):
    source = refs[0]
    out_ref, hot_ref, gate_ref = refs[1 + n_after :]

    @pl.when(pl.program_id(0) == 0)
    def _():
        hot, gate = slots_by_row(routing_ref[...], groups, block)
        hot_ref[...] = hot
        gate_ref[...] = jnp.broadcast_to(gate, gate_ref.shape)

    rows = dot(hot_ref[...], source[...])
    if gated:
        rows = (OUT_SCALE * gate_ref[:, :1]) * rows
    for k in range(groups):
        out_ref[k] = rows[k * block : (k + 1) * block].astype(BF16)


def dispatch(routing, source, groups, block, chunk, gated=False, wait_for=()):
    n_rows, width = source.shape
    return pl.pallas_call(
        functools.partial(dispatch_kernel, groups, block, gated, len(wait_for)),
        grid=(width // chunk,),
        in_specs=[
            pl.BlockSpec(routing.shape, lambda d: (0, 0)),
            pl.BlockSpec((n_rows, chunk), lambda d: (0, d)),
        ]
        + [pl.BlockSpec(memory_space=pl.ANY) for _ in wait_for],
        out_specs=pl.BlockSpec((groups, block, chunk), lambda d: (0, 0, d)),
        out_shape=jax.ShapeDtypeStruct((groups, block, width), BF16),
        scratch_shapes=[
            pltpu.VMEM((groups * block, n_rows), BF16),
            pltpu.VMEM((groups * block, 128), F32),
        ],
        compiler_params=params(),
        cost_estimate=SHORT,
        name="dispatch",
    )(routing, source, *wait_for)


def expert_kernel(n, n_chunks, backward, *refs):
    me_ref, rows_hbm, first_hbm, second_hbm = refs[:4]
    at = 7 if backward else 4
    outs = refs[at : at + n]
    sent_hbm, middle_ref = refs[at + n : at + n + 2]
    pre_ref = refs[4] if backward else refs[at + n + 2]
    rows_v, first_v, second_v, out_v, pre_v, middle_v, in_sem, out_sem, own_sem = refs[-9:]
    rows, width = rows_v.shape
    chunk = width // n_chunks
    columns = [pl.ds(d * chunk, chunk) for d in range(n_chunks)]

    def load(d):
        return [
            pltpu.make_async_copy(
                rows_hbm.at[:, columns[d]], rows_v.at[:, columns[d]], in_sem.at[0, d]
            ),
            pltpu.make_async_copy(first_hbm.at[columns[d]], first_v.at[columns[d]], in_sem.at[1, d]),
        ]

    def load_second(d):
        return pltpu.make_async_copy(
            second_hbm.at[columns[d]], second_v.at[columns[d]], in_sem.at[2, d]
        )

    def send(d):
        target = sent_hbm.at[d, pl.ds(rows if backward else 0, rows)]
        return pltpu.make_async_copy(rows_v.at[:, columns[d]], target, in_sem.at[3, d])

    def store(d, k):
        return pltpu.make_async_copy(
            out_v.at[me_ref[0] ^ k, :, columns[d]], outs[k].at[:, columns[d]], out_sem.at[d, k]
        )

    keep_middle = pltpu.make_async_copy(middle_v, middle_ref, own_sem.at[0])
    if backward:
        move_pre = pltpu.make_async_copy(pre_ref, pre_v, own_sem.at[1])
    else:
        move_pre = pltpu.make_async_copy(pre_v, pre_ref, own_sem.at[1])
    for d in range(n_chunks):
        for copy in load(d):
            copy.start()
    if backward:
        move_pre.start()
    for d in range(n_chunks):
        load_second(d).start()
    total = None
    for d in range(n_chunks):
        for copy in load(d):
            copy.wait()
        send(d).start()
        part = dot(rows_v[:, columns[d]], first_v[columns[d]])
        total = part if d == 0 else total + part
    if backward:
        move_pre.wait()
        middle = (total * gelu_slope(pre_v[...])).astype(BF16)
    else:
        pre_v[...] = total
        move_pre.start()
        middle = gelu(total).astype(BF16)
    middle_v[...] = middle
    keep_middle.start()
    for d in range(n_chunks):
        load_second(d).wait()
        result = contract_columns(middle, second_v[columns[d]])
        out_v[:, :, columns[d]] = result.reshape(n, rows // n, chunk).astype(BF16)
        for k in range(n):
            store(d, k).start()
    for d in range(n_chunks):
        send(d).wait()
        for k in range(n):
            store(d, k).wait()
    keep_middle.wait()
    if not backward:
        move_pre.wait()


def expert(me, rows_in, first, second, n_chunks, pre=None, sent=None, wait_for=None):
    n, block, width = rows_in.shape
    rows = n * block
    hidden = first.shape[1]
    chunk = width // n_chunks
    backward = pre is not None
    anywhere = pl.BlockSpec(memory_space=pl.ANY)
    operands = (me, rows_in.reshape(rows, width), first, second)
    in_specs = [pl.BlockSpec(memory_space=pltpu.SMEM)] + [anywhere] * 3
    if backward:
        operands += (pre, sent, wait_for)
        in_specs += [anywhere] * 3
    results = pl.pallas_call(
        functools.partial(expert_kernel, n, n_chunks, backward),
        in_specs=in_specs,
        out_specs=[anywhere] * (n + 2 if backward else n + 3),
        out_shape=[jax.ShapeDtypeStruct((block, width), BF16)] * n
        + [
            jax.ShapeDtypeStruct((n_chunks, 2 * rows, chunk), BF16),
            jax.ShapeDtypeStruct((rows, hidden), BF16),
        ]
        + ([] if backward else [jax.ShapeDtypeStruct((rows, hidden), F32)]),
        scratch_shapes=[
            pltpu.VMEM((rows, width), BF16),
            pltpu.VMEM((width, hidden), BF16),
            pltpu.VMEM((width, hidden), BF16),
            pltpu.VMEM((n, block, width), BF16),
            pltpu.VMEM((rows, hidden), F32),
            pltpu.VMEM((rows, hidden), BF16),
            pltpu.SemaphoreType.DMA((4, n_chunks)),
            pltpu.SemaphoreType.DMA((n_chunks, n)),
            pltpu.SemaphoreType.DMA((2,)),
        ],
        input_output_aliases={5: n} if backward else {},
        compiler_params=params(),
        cost_estimate=SHORT,
        name="expert_backward" if backward else "expert_forward",
    )(*operands)
    return (results[:n],) + tuple(results[n:])


def plan_kernel(groups, block, me_ref, routing_ref, hot_ref, sum_ref, gate_ref):
    hot, gates = slots_by_column(routing_ref[...], me_ref[0], groups, block)
    hot_ref[...] = jnp.concatenate(hot, axis=0)
    sum_ref[...] = (hot[0].astype(F32) + hot[1].astype(F32)).astype(BF16)
    for k in (0, 1):
        gate_ref[:, k * 128 : (k + 1) * 128] = jnp.broadcast_to(
            OUT_SCALE * gates[k], (gates[k].shape[0], 128)
        )


def plan(me, routing, groups, block, wait_for=()):
    n_rows = routing.shape[0]
    whole = pl.BlockSpec(memory_space=pltpu.VMEM)
    n_after = len(wait_for)

    def kernel(me_ref, routing_ref, *refs):
        plan_kernel(groups, block, me_ref, routing_ref, *refs[n_after:])

    return pl.pallas_call(
        kernel,
        in_specs=[pl.BlockSpec(memory_space=pltpu.SMEM), whole]
        + [pl.BlockSpec(memory_space=pl.ANY) for _ in wait_for],
        out_specs=[whole] * 3,
        out_shape=[
            jax.ShapeDtypeStruct((2 * n_rows, groups * block), BF16),
            jax.ShapeDtypeStruct((n_rows, groups * block), BF16),
            jax.ShapeDtypeStruct((n_rows, 256), F32),
        ],
        compiler_params=params(),
        cost_estimate=SHORT,
        name="plan",
    )(me, routing, *wait_for)


def combine_kernel(groups, gated, n_arrived, n_after, hot_ref, gate_ref, *refs):
    blocks = refs[:groups]
    arrived = refs[groups : groups + n_arrived]
    outs = refs[groups + n_arrived + n_after :]
    rows = stack([ref[...] for ref in blocks])
    n_rows = gate_ref.shape[0]
    total = dot(hot_ref[...], rows)
    if gated:
        total = gate_ref[:, :1] * total[:n_rows] + gate_ref[:, 128:129] * total[n_rows:]
    if arrived:
        total = total + jnp.concatenate([ref[...].astype(F32) for ref in arrived], axis=0)
    at = 0
    for ref in outs:
        ref[...] = total[at : at + ref.shape[0]].astype(BF16)
        at += ref.shape[0]


def combine(slots, blocks, chunk, gated=False, arrived=(), wait_for=(), parts=None):
    hot = slots[0] if gated else slots[1]
    gate = slots[2]
    n_rows = gate.shape[0]
    block, width = blocks[0].shape
    by_rows = lambda n: pl.BlockSpec((n, chunk), lambda d: (0, d))
    results = pl.pallas_call(
        functools.partial(combine_kernel, len(blocks), gated, len(arrived), len(wait_for)),
        grid=(width // chunk,),
        in_specs=[
            pl.BlockSpec(hot.shape, lambda d: (0, 0)),
            pl.BlockSpec(gate.shape, lambda d: (0, 0)),
        ]
        + [by_rows(block) for _ in blocks]
        + [by_rows(rows.shape[0]) for rows in arrived]
        + [pl.BlockSpec(memory_space=pl.ANY) for _ in wait_for],
        out_specs=[by_rows(n) for n in parts or (n_rows,)],
        out_shape=[jax.ShapeDtypeStruct((n, width), BF16) for n in parts or (n_rows,)],
        compiler_params=params(),
        cost_estimate=SHORT,
        name="combine",
    )(hot, gate, *blocks, *arrived, *wait_for)
    return results if parts else results[0]


def weight_kernel(n_dp, rows, traded_ref, pre_ref, hidden_ref, *outs):
    for i, factor_ref in enumerate((pre_ref, hidden_ref)):
        total = None
        for d in range(n_dp):
            part = contract_rows(
                traded_ref[d, i * rows : (i + 1) * rows, :],
                factor_ref[d * rows : (d + 1) * rows, :],
            )
            total = part if d == 0 else total + part
        outs[i][0] = total.astype(BF16)


def weight_grads(traded, pre_all, hidden_all, lanes):
    n_dp, depth, width = traded.shape
    hidden = pre_all.shape[1]
    whole = pl.BlockSpec(pre_all.shape, lambda i: (0, 0))
    return pl.pallas_call(
        functools.partial(weight_kernel, n_dp, depth // 2),
        grid=(width // lanes,),
        in_specs=[pl.BlockSpec((n_dp, depth, lanes), lambda i: (0, 0, i)), whole, whole],
        out_specs=[pl.BlockSpec((1, lanes, hidden), lambda i: (0, i, 0))] * 2,
        out_shape=[jax.ShapeDtypeStruct((1, width, hidden), BF16)] * 2,
        compiler_params=params(),
        cost_estimate=SHORT,
        name="weight_grads",
    )(traded, pre_all, hidden_all)


def after_kernel(*refs):
    pass


def after(values, *others):
    anywhere = pl.BlockSpec(memory_space=pl.ANY)
    return pl.pallas_call(
        after_kernel,
        in_specs=[anywhere] * (1 + len(others)),
        out_specs=anywhere,
        out_shape=jax.ShapeDtypeStruct(values.shape, values.dtype),
        input_output_aliases={0: 0},
        cost_estimate=SHORT,
        name="after",
    )(values, *others)


def permute_xor(values, axis, mask):
    size = lax.axis_size(axis)
    return lax.ppermute(values, axis, [(i, i ^ mask) for i in range(size)])


def exchange(blocks):
    return [blocks[0]] + [permute_xor(blocks[k], "expert", k) for k in range(1, len(blocks))]


def local(tokens, grad_out, expert_ids, gate_codes, w_up, w_down):
    n_expert = lax.axis_size("expert")
    n_dp = lax.axis_size("dp")
    n_rows, width = tokens.shape
    capacity = max(2, 12 * n_rows // (5 * n_expert))
    block = -(-capacity // ROW_TILE) * ROW_TILE
    half = n_expert // 2
    chunk = width // 2
    me = lax.axis_index("expert").astype(I32).reshape(1)

    def swap_direct(blocks):
        return lax.all_to_all(blocks, "expert", split_axis=0, concat_axis=0, tiled=True)

    routing = jnp.concatenate([expert_ids, gate_codes], axis=1)
    far_routing = permute_xor(routing, "expert", half)
    up_weight = lax.all_gather(w_up, "dp", axis=1, tiled=True)[0]
    down_weight = lax.all_gather(w_down, "dp", axis=1, tiled=True)[0]

    rows_out = dispatch(routing, tokens, n_expert, block, chunk)
    rows_in = swap_direct(rows_out)
    grads_out = dispatch(
        routing, grad_out, n_expert, block, chunk, gated=True, wait_for=(rows_out,)
    )
    grads_in = swap_direct(after(grads_out, far_routing))

    out, sent, hidden, pre_act = expert(me, rows_in, up_weight, down_weight, n_dp)
    parts = (n_rows // 4, n_rows - n_rows // 4)
    far_out = exchange(out[half:])
    far_slots = plan(me, far_routing, half, block, (out[0],))
    near_slots = plan(me, routing, half, block, (out[0],))
    far_mixed = combine(far_slots, far_out, chunk, gated=True, parts=parts)
    near_back = exchange(out[:half])
    mixed_in = [permute_xor(far_mixed[0], "expert", half)]
    mixed_in.append(permute_xor(after(far_mixed[1], mixed_in[0]), "expert", half))

    row_grads, sent, pre_grad = expert(
        me, grads_in, down_weight, up_weight, n_dp, pre=pre_act, sent=sent, wait_for=far_mixed[0]
    )
    ready = (mixed_in[0], *near_back[1:])
    far_back = exchange([after(rows, *ready) for rows in row_grads[half:]])
    far_sum = combine(far_slots, far_back, chunk, wait_for=(mixed_in[1],))
    sum_in = permute_xor(far_sum, "expert", half)
    near_grad = exchange([after(rows, far_sum) for rows in row_grads[:half]])
    traded = lax.all_to_all(
        after(sent, *ready), "dp", split_axis=0, concat_axis=0, tiled=True
    )
    hidden_all = lax.all_gather(hidden, "dp", axis=0, tiled=True)
    pre_all = lax.all_gather(after(pre_grad, *ready), "dp", axis=0, tiled=True)

    grad_up, grad_down = weight_grads(traded, pre_all, hidden_all, 256)
    layer_output = combine(
        near_slots,
        near_back,
        chunk,
        gated=True,
        arrived=mixed_in,
        wait_for=(grad_up, grad_down),
    )
    grad_tokens = combine(
        near_slots, near_grad, chunk, arrived=(sum_in,), wait_for=(layer_output,)
    )
    return (layer_output, grad_tokens, grad_up, grad_down)


def solution(mesh):
    in_specs = (
        P(("dp", "expert"), None),
        P(("dp", "expert"), None),
        P(("dp", "expert"), None),
        P(("dp", "expert"), None),
        P("expert", "dp", None),
        P("expert", "dp", None),
    )
    out_specs = (
        P(("dp", "expert"), None),
        P(("dp", "expert"), None),
        P("expert", "dp", None),
        P("expert", "dp", None),
    )
    return jax.shard_map(local, mesh=mesh, in_specs=in_specs, out_specs=out_specs, check_vma=False)
```

```python
import functools
import math

import jax
import jax.numpy as jnp
from jax import lax
from jax.experimental import pallas as pl
from jax.experimental.pallas import tpu as pltpu
from jax.sharding import PartitionSpec as P

LAYERS = 40
OUT_SCALE = 1.0 / math.sqrt(2.0 * LAYERS)
ROW_TILE = 8
VMEM_LIMIT = 64 * 1024 * 1024 - 65536
F32, BF16, I32 = jnp.float32, jnp.bfloat16, jnp.int32
GELU_SCALE = math.sqrt(2.0 / math.pi)
GELU_CUBE = 0.044715


def dot(former, latter):
    return jnp.dot(former, latter, preferred_element_type=F32)


def contract_rows(former, latter):
    return lax.dot_general(former, latter, (((0,), (0,)), ((), ())), preferred_element_type=F32)


def contract_columns(former, latter):
    return lax.dot_general(former, latter, (((1,), (1,)), ((), ())), preferred_element_type=F32)


def iota(shape, dim):
    return lax.broadcasted_iota(I32, shape, dim)


def as_bf16(condition):
    return jnp.where(condition, 1.0, 0.0).astype(BF16)


def gelu(v):
    t = jnp.tanh(GELU_SCALE * (v + GELU_CUBE * (v * v * v)))
    return v * (0.5 * (1.0 + t))


def gelu_slope(v):
    t = jnp.tanh(GELU_SCALE * (v + GELU_CUBE * (v * v * v)))
    inner = GELU_SCALE * (1.0 + 3.0 * GELU_CUBE * (v * v))
    return 0.5 * (1.0 + t) + 0.5 * v * (1.0 - t * t) * inner


def stack(pieces):
    return jnp.concatenate([piece.astype(F32) for piece in pieces], axis=0).astype(BF16)


SHORT = pl.CostEstimate(flops=1, bytes_accessed=1, transcendentals=0)


def params(**kwargs):
    return pltpu.CompilerParams(vmem_limit_bytes=VMEM_LIMIT, **kwargs)


def slots_by_row(routing, half, block):
    n_rows = routing.shape[0]
    lane = iota((n_rows, 128), 1)
    wide = jnp.zeros((n_rows, 128), F32)
    for k in range(4):
        wide = jnp.where(lane == k, routing[:, k : k + 1].astype(F32), wide)
    turned = wide.T
    ids = [turned[k : k + 1, :].astype(I32) for k in (0, 1)]
    codes = [turned[k : k + 1, :] for k in (2, 3)]
    total = codes[0] + codes[1]
    gates = [code / total for code in codes]
    height = -(-half // 8) * 8
    expert = iota((height, n_rows), 0)
    named = [ids[k] == expert for k in (0, 1)]
    either = named[0] | named[1]
    earlier = as_bf16(iota((n_rows, n_rows), 0) < iota((n_rows, n_rows), 1))
    before = dot(as_bf16(either), earlier)
    before = jnp.where(either, before, -1.0)
    gate = jnp.where(named[0], gates[0], jnp.where(named[1], gates[1], 0.0))
    place = iota((block, n_rows), 0).astype(F32)
    hot = [jnp.where(place == before[k : k + 1, :], 1.0, 0.0) for k in range(half)]
    slot_gates = [
        jnp.sum(hot[k] * gate[k : k + 1, :], axis=1, keepdims=True) for k in range(half)
    ]
    return jnp.concatenate(hot, axis=0).astype(BF16), jnp.concatenate(slot_gates, axis=0)


def slots_by_column(routing, me, half, block):
    n_rows = routing.shape[0]
    n_slots = half * block
    ids = [routing[:, k : k + 1] for k in (0, 1)]
    codes = [routing[:, k : k + 1].astype(F32) for k in (2, 3)]
    total = codes[0] + codes[1]
    gates = [code / total for code in codes]
    lanes = 128
    expert = me ^ iota((n_rows, lanes), 1)
    within = iota((n_rows, lanes), 1) < half
    either = ((ids[0] == expert) | (ids[1] == expert)) & within
    earlier = as_bf16(iota((n_rows, n_rows), 1) < iota((n_rows, n_rows), 0))
    before = dot(earlier, as_bf16(either))
    slot = iota((lanes, n_slots), 1)
    owner = iota((lanes, n_slots), 0)
    spread = as_bf16((slot >= owner * block) & (slot < (owner + 1) * block))
    before = dot(before.astype(BF16), spread)
    number = dot(as_bf16(iota((n_rows, lanes), 1) >= 0), as_bf16(slot >= (owner + 1) * block))
    slot_row = iota((n_rows, n_slots), 1)
    owner_row = number.astype(I32)
    place = (slot_row - owner_row * block).astype(F32) == before
    slot_expert = me ^ owner_row
    hot = [as_bf16((ids[k] == slot_expert) & place) for k in (0, 1)]
    return hot, gates


def dispatch_kernel(groups, block, gated, n_after, routing_ref, *refs):
    source = refs[0]
    out_ref, hot_ref, gate_ref = refs[1 + n_after :]

    @pl.when(pl.program_id(0) == 0)
    def _():
        hot, gate = slots_by_row(routing_ref[...], groups, block)
        hot_ref[...] = hot
        gate_ref[...] = jnp.broadcast_to(gate, gate_ref.shape)

    rows = dot(hot_ref[...], source[...])
    if gated:
        rows = (OUT_SCALE * gate_ref[:, :1]) * rows
    for k in range(groups):
        out_ref[k] = rows[k * block : (k + 1) * block].astype(BF16)


def dispatch(routing, source, groups, block, chunk, gated=False, wait_for=()):
    n_rows, width = source.shape
    return pl.pallas_call(
        functools.partial(dispatch_kernel, groups, block, gated, len(wait_for)),
        grid=(width // chunk,),
        in_specs=[
            pl.BlockSpec(routing.shape, lambda d: (0, 0)),
            pl.BlockSpec((n_rows, chunk), lambda d: (0, d)),
        ]
        + [pl.BlockSpec(memory_space=pl.ANY) for _ in wait_for],
        out_specs=pl.BlockSpec((groups, block, chunk), lambda d: (0, 0, d)),
        out_shape=jax.ShapeDtypeStruct((groups, block, width), BF16),
        scratch_shapes=[
            pltpu.VMEM((groups * block, n_rows), BF16),
            pltpu.VMEM((groups * block, 128), F32),
        ],
        compiler_params=params(),
        cost_estimate=SHORT,
        name="dispatch",
    )(routing, source, *wait_for)


def expert_kernel(n, n_chunks, backward, *refs):
    me_ref, rows_hbm, first_hbm, second_hbm = refs[:4]
    at = 7 if backward else 4
    outs = refs[at : at + n]
    sent_hbm, middle_ref = refs[at + n : at + n + 2]
    pre_ref = refs[4] if backward else refs[at + n + 2]
    rows_v, first_v, second_v, out_v, pre_v, middle_v, in_sem, out_sem, own_sem = refs[-9:]
    rows, width = rows_v.shape
    chunk = width // n_chunks
    columns = [pl.ds(d * chunk, chunk) for d in range(n_chunks)]

    def load(d):
        return [
            pltpu.make_async_copy(
                rows_hbm.at[:, columns[d]], rows_v.at[:, columns[d]], in_sem.at[0, d]
            ),
            pltpu.make_async_copy(first_hbm.at[columns[d]], first_v.at[columns[d]], in_sem.at[1, d]),
        ]

    def load_second(d):
        return pltpu.make_async_copy(
            second_hbm.at[columns[d]], second_v.at[columns[d]], in_sem.at[2, d]
        )

    def send(d):
        target = sent_hbm.at[d, pl.ds(rows if backward else 0, rows)]
        return pltpu.make_async_copy(rows_v.at[:, columns[d]], target, in_sem.at[3, d])

    def store(d, k):
        return pltpu.make_async_copy(
            out_v.at[me_ref[0] ^ k, :, columns[d]], outs[k].at[:, columns[d]], out_sem.at[d, k]
        )

    keep_middle = pltpu.make_async_copy(middle_v, middle_ref, own_sem.at[0])
    if backward:
        move_pre = pltpu.make_async_copy(pre_ref, pre_v, own_sem.at[1])
    else:
        move_pre = pltpu.make_async_copy(pre_v, pre_ref, own_sem.at[1])
    for d in range(n_chunks):
        for copy in load(d):
            copy.start()
    if backward:
        move_pre.start()
    for d in range(n_chunks):
        load_second(d).start()
    total = None
    for d in range(n_chunks):
        for copy in load(d):
            copy.wait()
        send(d).start()
        part = dot(rows_v[:, columns[d]], first_v[columns[d]])
        total = part if d == 0 else total + part
    if backward:
        move_pre.wait()
        middle = (total * gelu_slope(pre_v[...])).astype(BF16)
    else:
        pre_v[...] = total
        move_pre.start()
        middle = gelu(total).astype(BF16)
    middle_v[...] = middle
    keep_middle.start()
    for d in range(n_chunks):
        load_second(d).wait()
        result = contract_columns(middle, second_v[columns[d]])
        out_v[:, :, columns[d]] = result.reshape(n, rows // n, chunk).astype(BF16)
        for k in range(n):
            store(d, k).start()
    for d in range(n_chunks):
        send(d).wait()
        for k in range(n):
            store(d, k).wait()
    keep_middle.wait()
    if not backward:
        move_pre.wait()


def expert(me, rows_in, first, second, n_chunks, pre=None, sent=None, wait_for=None):
    n, block, width = rows_in.shape
    rows = n * block
    hidden = first.shape[1]
    chunk = width // n_chunks
    backward = pre is not None
    anywhere = pl.BlockSpec(memory_space=pl.ANY)
    operands = (me, rows_in.reshape(rows, width), first, second)
    in_specs = [pl.BlockSpec(memory_space=pltpu.SMEM)] + [anywhere] * 3
    if backward:
        operands += (pre, sent, wait_for)
        in_specs += [anywhere] * 3
    results = pl.pallas_call(
        functools.partial(expert_kernel, n, n_chunks, backward),
        in_specs=in_specs,
        out_specs=[anywhere] * (n + 2 if backward else n + 3),
        out_shape=[jax.ShapeDtypeStruct((block, width), BF16)] * n
        + [
            jax.ShapeDtypeStruct((n_chunks, 2 * rows, chunk), BF16),
            jax.ShapeDtypeStruct((rows, hidden), BF16),
        ]
        + ([] if backward else [jax.ShapeDtypeStruct((rows, hidden), F32)]),
        scratch_shapes=[
            pltpu.VMEM((rows, width), BF16),
            pltpu.VMEM((width, hidden), BF16),
            pltpu.VMEM((width, hidden), BF16),
            pltpu.VMEM((n, block, width), BF16),
            pltpu.VMEM((rows, hidden), F32),
            pltpu.VMEM((rows, hidden), BF16),
            pltpu.SemaphoreType.DMA((4, n_chunks)),
            pltpu.SemaphoreType.DMA((n_chunks, n)),
            pltpu.SemaphoreType.DMA((2,)),
        ],
        input_output_aliases={5: n} if backward else {},
        compiler_params=params(),
        cost_estimate=SHORT,
        name="expert_backward" if backward else "expert_forward",
    )(*operands)
    return (results[:n],) + tuple(results[n:])


def plan_kernel(groups, block, me_ref, routing_ref, hot_ref, sum_ref, gate_ref):
    hot, gates = slots_by_column(routing_ref[...], me_ref[0], groups, block)
    hot_ref[...] = jnp.concatenate(hot, axis=0)
    sum_ref[...] = (hot[0].astype(F32) + hot[1].astype(F32)).astype(BF16)
    for k in (0, 1):
        gate_ref[:, k * 128 : (k + 1) * 128] = jnp.broadcast_to(
            OUT_SCALE * gates[k], (gates[k].shape[0], 128)
        )


def plan(me, routing, groups, block, wait_for=()):
    n_rows = routing.shape[0]
    whole = pl.BlockSpec(memory_space=pltpu.VMEM)
    n_after = len(wait_for)

    def kernel(me_ref, routing_ref, *refs):
        plan_kernel(groups, block, me_ref, routing_ref, *refs[n_after:])

    return pl.pallas_call(
        kernel,
        in_specs=[pl.BlockSpec(memory_space=pltpu.SMEM), whole]
        + [pl.BlockSpec(memory_space=pl.ANY) for _ in wait_for],
        out_specs=[whole] * 3,
        out_shape=[
            jax.ShapeDtypeStruct((2 * n_rows, groups * block), BF16),
            jax.ShapeDtypeStruct((n_rows, groups * block), BF16),
            jax.ShapeDtypeStruct((n_rows, 256), F32),
        ],
        compiler_params=params(),
        cost_estimate=SHORT,
        name="plan",
    )(me, routing, *wait_for)


def combine_kernel(groups, gated, n_arrived, n_after, hot_ref, gate_ref, *refs):
    blocks = refs[:groups]
    arrived = refs[groups : groups + n_arrived]
    outs = refs[groups + n_arrived + n_after :]
    rows = stack([ref[...] for ref in blocks])
    n_rows = gate_ref.shape[0]
    total = dot(hot_ref[...], rows)
    if gated:
        total = gate_ref[:, :1] * total[:n_rows] + gate_ref[:, 128:129] * total[n_rows:]
    if arrived:
        total = total + jnp.concatenate([ref[...].astype(F32) for ref in arrived], axis=0)
    at = 0
    for ref in outs:
        ref[...] = total[at : at + ref.shape[0]].astype(BF16)
        at += ref.shape[0]


def combine(slots, blocks, chunk, gated=False, arrived=(), wait_for=(), parts=None):
    hot = slots[0] if gated else slots[1]
    gate = slots[2]
    n_rows = gate.shape[0]
    block, width = blocks[0].shape
    by_rows = lambda n: pl.BlockSpec((n, chunk), lambda d: (0, d))
    results = pl.pallas_call(
        functools.partial(combine_kernel, len(blocks), gated, len(arrived), len(wait_for)),
        grid=(width // chunk,),
        in_specs=[
            pl.BlockSpec(hot.shape, lambda d: (0, 0)),
            pl.BlockSpec(gate.shape, lambda d: (0, 0)),
        ]
        + [by_rows(block) for _ in blocks]
        + [by_rows(rows.shape[0]) for rows in arrived]
        + [pl.BlockSpec(memory_space=pl.ANY) for _ in wait_for],
        out_specs=[by_rows(n) for n in parts or (n_rows,)],
        out_shape=[jax.ShapeDtypeStruct((n, width), BF16) for n in parts or (n_rows,)],
        compiler_params=params(),
        cost_estimate=SHORT,
        name="combine",
    )(hot, gate, *blocks, *arrived, *wait_for)
    return results if parts else results[0]


def weight_kernel(n_dp, rows, traded_ref, pre_ref, hidden_ref, *outs):
    for i, factor_ref in enumerate((pre_ref, hidden_ref)):
        total = None
        for d in range(n_dp):
            part = contract_rows(
                traded_ref[d, i * rows : (i + 1) * rows, :],
                factor_ref[d * rows : (d + 1) * rows, :],
            )
            total = part if d == 0 else total + part
        outs[i][0] = total.astype(BF16)


def weight_grads(traded, pre_all, hidden_all, lanes):
    n_dp, depth, width = traded.shape
    hidden = pre_all.shape[1]
    whole = pl.BlockSpec(pre_all.shape, lambda i: (0, 0))
    return pl.pallas_call(
        functools.partial(weight_kernel, n_dp, depth // 2),
        grid=(width // lanes,),
        in_specs=[pl.BlockSpec((n_dp, depth, lanes), lambda i: (0, 0, i)), whole, whole],
        out_specs=[pl.BlockSpec((1, lanes, hidden), lambda i: (0, i, 0))] * 2,
        out_shape=[jax.ShapeDtypeStruct((1, width, hidden), BF16)] * 2,
        compiler_params=params(),
        cost_estimate=SHORT,
        name="weight_grads",
    )(traded, pre_all, hidden_all)


def after_kernel(*refs):
    pass


def after(values, *others):
    anywhere = pl.BlockSpec(memory_space=pl.ANY)
    return pl.pallas_call(
        after_kernel,
        in_specs=[anywhere] * (1 + len(others)),
        out_specs=anywhere,
        out_shape=jax.ShapeDtypeStruct(values.shape, values.dtype),
        input_output_aliases={0: 0},
        cost_estimate=SHORT,
        name="after",
    )(values, *others)


def permute_xor(values, axis, mask):
    size = lax.axis_size(axis)
    return lax.ppermute(values, axis, [(i, i ^ mask) for i in range(size)])


def exchange(blocks):
    return [blocks[0]] + [permute_xor(blocks[k], "expert", k) for k in range(1, len(blocks))]


def local(tokens, grad_out, expert_ids, gate_codes, w_up, w_down):
    n_expert = lax.axis_size("expert")
    n_dp = lax.axis_size("dp")
    n_rows, width = tokens.shape
    capacity = max(2, 12 * n_rows // (5 * n_expert))
    block = -(-capacity // ROW_TILE) * ROW_TILE
    half = n_expert // 2
    chunk = width // 2
    me = lax.axis_index("expert").astype(I32).reshape(1)

    def swap_direct(blocks):
        return lax.all_to_all(blocks, "expert", split_axis=0, concat_axis=0, tiled=True)

    routing = jnp.concatenate([expert_ids, gate_codes], axis=1)
    far_routing = permute_xor(routing, "expert", half)
    up_weight = lax.all_gather(w_up, "dp", axis=1, tiled=True)[0]
    down_weight = lax.all_gather(w_down, "dp", axis=1, tiled=True)[0]

    rows_out = dispatch(routing, tokens, n_expert, block, chunk)
    rows_in = swap_direct(rows_out)
    grads_out = dispatch(
        routing, grad_out, n_expert, block, chunk, gated=True, wait_for=(rows_out,)
    )
    grads_in = swap_direct(after(grads_out, far_routing))

    out, sent, hidden, pre_act = expert(me, rows_in, up_weight, down_weight, n_dp)
    parts = (n_rows // 4, n_rows - n_rows // 4)
    far_out = exchange(out[half:])
    far_slots = plan(me, far_routing, half, block, (out[0],))
    near_slots = plan(me, routing, half, block, (out[0],))
    far_mixed = combine(far_slots, far_out, chunk, gated=True, parts=parts)
    near_back = exchange(out[:half])
    mixed_in = [permute_xor(far_mixed[0], "expert", half)]
    mixed_in.append(permute_xor(after(far_mixed[1], mixed_in[0]), "expert", half))

    row_grads, sent, pre_grad = expert(
        me, grads_in, down_weight, up_weight, n_dp, pre=pre_act, sent=sent, wait_for=far_mixed[0]
    )
    ready = (mixed_in[0], *near_back[1:])
    far_back = exchange([after(rows, *ready) for rows in row_grads[half:]])
    far_sum = combine(far_slots, far_back, chunk)
    sum_in = permute_xor(after(far_sum, mixed_in[1]), "expert", half)
    near_grad = exchange([after(rows, far_sum) for rows in row_grads[:half]])
    traded = lax.all_to_all(
        after(sent, *ready), "dp", split_axis=0, concat_axis=0, tiled=True
    )
    hidden_all = lax.all_gather(hidden, "dp", axis=0, tiled=True)
    pre_all = lax.all_gather(after(pre_grad, *ready), "dp", axis=0, tiled=True)

    grad_up, grad_down = weight_grads(traded, pre_all, hidden_all, 256)
    layer_output = combine(
        near_slots,
        near_back,
        chunk,
        gated=True,
        arrived=mixed_in,
        wait_for=(grad_up, grad_down),
    )
    grad_tokens = combine(
        near_slots, near_grad, chunk, arrived=(sum_in,), wait_for=(layer_output,)
    )
    return (layer_output, grad_tokens, grad_up, grad_down)


def solution(mesh):
    in_specs = (
        P(("dp", "expert"), None),
        P(("dp", "expert"), None),
        P(("dp", "expert"), None),
        P(("dp", "expert"), None),
        P("expert", "dp", None),
        P("expert", "dp", None),
    )
    out_specs = (
        P(("dp", "expert"), None),
        P(("dp", "expert"), None),
        P("expert", "dp", None),
        P("expert", "dp", None),
    )
    return jax.shard_map(local, mesh=mesh, in_specs=in_specs, out_specs=out_specs, check_vma=False)
```

```python
import functools
import math

import jax
import jax.numpy as jnp
from jax import lax
from jax.experimental import pallas as pl
from jax.experimental.pallas import tpu as pltpu
from jax.sharding import PartitionSpec as P

LAYERS = 40
OUT_SCALE = 1.0 / math.sqrt(2.0 * LAYERS)
ROW_TILE = 8
VMEM_LIMIT = 64 * 1024 * 1024 - 65536
F32, BF16, I32 = jnp.float32, jnp.bfloat16, jnp.int32
GELU_SCALE = math.sqrt(2.0 / math.pi)
GELU_CUBE = 0.044715


def dot(former, latter):
    return jnp.dot(former, latter, preferred_element_type=F32)


def contract_rows(former, latter):
    return lax.dot_general(former, latter, (((0,), (0,)), ((), ())), preferred_element_type=F32)


def contract_columns(former, latter):
    return lax.dot_general(former, latter, (((1,), (1,)), ((), ())), preferred_element_type=F32)


def iota(shape, dim):
    return lax.broadcasted_iota(I32, shape, dim)


def as_bf16(condition):
    return jnp.where(condition, 1.0, 0.0).astype(BF16)


def gelu(v):
    t = jnp.tanh(GELU_SCALE * (v + GELU_CUBE * (v * v * v)))
    return v * (0.5 * (1.0 + t))


def gelu_slope(v):
    t = jnp.tanh(GELU_SCALE * (v + GELU_CUBE * (v * v * v)))
    inner = GELU_SCALE * (1.0 + 3.0 * GELU_CUBE * (v * v))
    return 0.5 * (1.0 + t) + 0.5 * v * (1.0 - t * t) * inner


def stack(pieces):
    return jnp.concatenate([piece.astype(F32) for piece in pieces], axis=0).astype(BF16)


SHORT = pl.CostEstimate(flops=1, bytes_accessed=1, transcendentals=0)


def params(**kwargs):
    return pltpu.CompilerParams(vmem_limit_bytes=VMEM_LIMIT, **kwargs)


def slots_by_row(routing, half, block):
    n_rows = routing.shape[0]
    lane = iota((n_rows, 128), 1)
    wide = jnp.zeros((n_rows, 128), F32)
    for k in range(4):
        wide = jnp.where(lane == k, routing[:, k : k + 1].astype(F32), wide)
    turned = wide.T
    ids = [turned[k : k + 1, :].astype(I32) for k in (0, 1)]
    codes = [turned[k : k + 1, :] for k in (2, 3)]
    total = codes[0] + codes[1]
    gates = [code / total for code in codes]
    height = -(-half // 8) * 8
    expert = iota((height, n_rows), 0)
    named = [ids[k] == expert for k in (0, 1)]
    either = named[0] | named[1]
    earlier = as_bf16(iota((n_rows, n_rows), 0) < iota((n_rows, n_rows), 1))
    before = dot(as_bf16(either), earlier)
    before = jnp.where(either, before, -1.0)
    gate = jnp.where(named[0], gates[0], jnp.where(named[1], gates[1], 0.0))
    place = iota((block, n_rows), 0).astype(F32)
    hot = [jnp.where(place == before[k : k + 1, :], 1.0, 0.0) for k in range(half)]
    slot_gates = [
        jnp.sum(hot[k] * gate[k : k + 1, :], axis=1, keepdims=True) for k in range(half)
    ]
    return jnp.concatenate(hot, axis=0).astype(BF16), jnp.concatenate(slot_gates, axis=0)


def slots_by_column(routing, me, half, block):
    n_rows = routing.shape[0]
    n_slots = half * block
    ids = [routing[:, k : k + 1] for k in (0, 1)]
    codes = [routing[:, k : k + 1].astype(F32) for k in (2, 3)]
    total = codes[0] + codes[1]
    gates = [code / total for code in codes]
    lanes = 128
    expert = me ^ iota((n_rows, lanes), 1)
    within = iota((n_rows, lanes), 1) < half
    either = ((ids[0] == expert) | (ids[1] == expert)) & within
    earlier = as_bf16(iota((n_rows, n_rows), 1) < iota((n_rows, n_rows), 0))
    before = dot(earlier, as_bf16(either))
    slot = iota((lanes, n_slots), 1)
    owner = iota((lanes, n_slots), 0)
    spread = as_bf16((slot >= owner * block) & (slot < (owner + 1) * block))
    before = dot(before.astype(BF16), spread)
    number = dot(as_bf16(iota((n_rows, lanes), 1) >= 0), as_bf16(slot >= (owner + 1) * block))
    slot_row = iota((n_rows, n_slots), 1)
    owner_row = number.astype(I32)
    place = (slot_row - owner_row * block).astype(F32) == before
    slot_expert = me ^ owner_row
    hot = [as_bf16((ids[k] == slot_expert) & place) for k in (0, 1)]
    return hot, gates


def dispatch_kernel(groups, block, gated, n_after, routing_ref, *refs):
    source = refs[0]
    out_ref, hot_ref, gate_ref = refs[1 + n_after :]

    @pl.when(pl.program_id(0) == 0)
    def _():
        hot, gate = slots_by_row(routing_ref[...], groups, block)
        hot_ref[...] = hot
        gate_ref[...] = jnp.broadcast_to(gate, gate_ref.shape)

    rows = dot(hot_ref[...], source[...])
    if gated:
        rows = (OUT_SCALE * gate_ref[:, :1]) * rows
    for k in range(groups):
        out_ref[k] = rows[k * block : (k + 1) * block].astype(BF16)


def dispatch(routing, source, groups, block, chunk, gated=False, wait_for=()):
    n_rows, width = source.shape
    return pl.pallas_call(
        functools.partial(dispatch_kernel, groups, block, gated, len(wait_for)),
        grid=(width // chunk,),
        in_specs=[
            pl.BlockSpec(routing.shape, lambda d: (0, 0)),
            pl.BlockSpec((n_rows, chunk), lambda d: (0, d)),
        ]
        + [pl.BlockSpec(memory_space=pl.ANY) for _ in wait_for],
        out_specs=pl.BlockSpec((groups, block, chunk), lambda d: (0, 0, d)),
        out_shape=jax.ShapeDtypeStruct((groups, block, width), BF16),
        scratch_shapes=[
            pltpu.VMEM((groups * block, n_rows), BF16),
            pltpu.VMEM((groups * block, 128), F32),
        ],
        compiler_params=params(),
        cost_estimate=SHORT,
        name="dispatch",
    )(routing, source, *wait_for)


def expert_kernel(n, n_chunks, backward, *refs):
    me_ref, rows_hbm, first_hbm, second_hbm = refs[:4]
    at = 7 if backward else 4
    outs = refs[at : at + n]
    sent_hbm, middle_ref = refs[at + n : at + n + 2]
    pre_ref = refs[4] if backward else refs[at + n + 2]
    rows_v, first_v, second_v, out_v, pre_v, middle_v, in_sem, out_sem, own_sem = refs[-9:]
    rows, width = rows_v.shape
    chunk = width // n_chunks
    columns = [pl.ds(d * chunk, chunk) for d in range(n_chunks)]

    def load(d):
        return [
            pltpu.make_async_copy(
                rows_hbm.at[:, columns[d]], rows_v.at[:, columns[d]], in_sem.at[0, d]
            ),
            pltpu.make_async_copy(first_hbm.at[columns[d]], first_v.at[columns[d]], in_sem.at[1, d]),
        ]

    def load_second(d):
        return pltpu.make_async_copy(
            second_hbm.at[columns[d]], second_v.at[columns[d]], in_sem.at[2, d]
        )

    def send(d):
        target = sent_hbm.at[d, pl.ds(rows if backward else 0, rows)]
        return pltpu.make_async_copy(rows_v.at[:, columns[d]], target, in_sem.at[3, d])

    def store(d, k):
        return pltpu.make_async_copy(
            out_v.at[me_ref[0] ^ k, :, columns[d]], outs[k].at[:, columns[d]], out_sem.at[d, k]
        )

    keep_middle = pltpu.make_async_copy(middle_v, middle_ref, own_sem.at[0])
    if backward:
        move_pre = pltpu.make_async_copy(pre_ref, pre_v, own_sem.at[1])
    else:
        move_pre = pltpu.make_async_copy(pre_v, pre_ref, own_sem.at[1])
    for d in range(n_chunks):
        for copy in load(d):
            copy.start()
    if backward:
        move_pre.start()
    for d in range(n_chunks):
        load_second(d).start()
    total = None
    for d in range(n_chunks):
        for copy in load(d):
            copy.wait()
        send(d).start()
        part = dot(rows_v[:, columns[d]], first_v[columns[d]])
        total = part if d == 0 else total + part
    if backward:
        move_pre.wait()
        middle = (total * gelu_slope(pre_v[...])).astype(BF16)
    else:
        pre_v[...] = total
        move_pre.start()
        middle = gelu(total).astype(BF16)
    middle_v[...] = middle
    keep_middle.start()
    for d in range(n_chunks):
        load_second(d).wait()
        result = contract_columns(middle, second_v[columns[d]])
        out_v[:, :, columns[d]] = result.reshape(n, rows // n, chunk).astype(BF16)
        for k in range(n):
            store(d, k).start()
    for d in range(n_chunks):
        send(d).wait()
        for k in range(n):
            store(d, k).wait()
    keep_middle.wait()
    if not backward:
        move_pre.wait()


def expert(me, rows_in, first, second, n_chunks, pre=None, sent=None, wait_for=None):
    n, block, width = rows_in.shape
    rows = n * block
    hidden = first.shape[1]
    chunk = width // n_chunks
    backward = pre is not None
    anywhere = pl.BlockSpec(memory_space=pl.ANY)
    operands = (me, rows_in.reshape(rows, width), first, second)
    in_specs = [pl.BlockSpec(memory_space=pltpu.SMEM)] + [anywhere] * 3
    if backward:
        operands += (pre, sent, wait_for)
        in_specs += [anywhere] * 3
    results = pl.pallas_call(
        functools.partial(expert_kernel, n, n_chunks, backward),
        in_specs=in_specs,
        out_specs=[anywhere] * (n + 2 if backward else n + 3),
        out_shape=[jax.ShapeDtypeStruct((block, width), BF16)] * n
        + [
            jax.ShapeDtypeStruct((n_chunks, 2 * rows, chunk), BF16),
            jax.ShapeDtypeStruct((rows, hidden), BF16),
        ]
        + ([] if backward else [jax.ShapeDtypeStruct((rows, hidden), F32)]),
        scratch_shapes=[
            pltpu.VMEM((rows, width), BF16),
            pltpu.VMEM((width, hidden), BF16),
            pltpu.VMEM((width, hidden), BF16),
            pltpu.VMEM((n, block, width), BF16),
            pltpu.VMEM((rows, hidden), F32),
            pltpu.VMEM((rows, hidden), BF16),
            pltpu.SemaphoreType.DMA((4, n_chunks)),
            pltpu.SemaphoreType.DMA((n_chunks, n)),
            pltpu.SemaphoreType.DMA((2,)),
        ],
        input_output_aliases={5: n} if backward else {},
        compiler_params=params(),
        cost_estimate=SHORT,
        name="expert_backward" if backward else "expert_forward",
    )(*operands)
    return (results[:n],) + tuple(results[n:])


def plan_kernel(groups, block, me_ref, routing_ref, hot_ref, sum_ref, gate_ref):
    hot, gates = slots_by_column(routing_ref[...], me_ref[0], groups, block)
    hot_ref[...] = jnp.concatenate(hot, axis=0)
    sum_ref[...] = (hot[0].astype(F32) + hot[1].astype(F32)).astype(BF16)
    for k in (0, 1):
        gate_ref[:, k * 128 : (k + 1) * 128] = jnp.broadcast_to(
            OUT_SCALE * gates[k], (gates[k].shape[0], 128)
        )


def plan(me, routing, groups, block, wait_for=()):
    n_rows = routing.shape[0]
    whole = pl.BlockSpec(memory_space=pltpu.VMEM)
    n_after = len(wait_for)

    def kernel(me_ref, routing_ref, *refs):
        plan_kernel(groups, block, me_ref, routing_ref, *refs[n_after:])

    return pl.pallas_call(
        kernel,
        in_specs=[pl.BlockSpec(memory_space=pltpu.SMEM), whole]
        + [pl.BlockSpec(memory_space=pl.ANY) for _ in wait_for],
        out_specs=[whole] * 3,
        out_shape=[
            jax.ShapeDtypeStruct((2 * n_rows, groups * block), BF16),
            jax.ShapeDtypeStruct((n_rows, groups * block), BF16),
            jax.ShapeDtypeStruct((n_rows, 256), F32),
        ],
        compiler_params=params(),
        cost_estimate=SHORT,
        name="plan",
    )(me, routing, *wait_for)


def combine_kernel(groups, gated, n_arrived, n_after, hot_ref, gate_ref, *refs):
    blocks = refs[:groups]
    arrived = refs[groups : groups + n_arrived]
    outs = refs[groups + n_arrived + n_after :]
    rows = stack([ref[...] for ref in blocks])
    n_rows = gate_ref.shape[0]
    total = dot(hot_ref[...], rows)
    if gated:
        total = gate_ref[:, :1] * total[:n_rows] + gate_ref[:, 128:129] * total[n_rows:]
    if arrived:
        total = total + jnp.concatenate([ref[...].astype(F32) for ref in arrived], axis=0)
    at = 0
    for ref in outs:
        ref[...] = total[at : at + ref.shape[0]].astype(BF16)
        at += ref.shape[0]


def combine(slots, blocks, chunk, gated=False, arrived=(), wait_for=(), parts=None):
    hot = slots[0] if gated else slots[1]
    gate = slots[2]
    n_rows = gate.shape[0]
    block, width = blocks[0].shape
    by_rows = lambda n: pl.BlockSpec((n, chunk), lambda d: (0, d))
    results = pl.pallas_call(
        functools.partial(combine_kernel, len(blocks), gated, len(arrived), len(wait_for)),
        grid=(width // chunk,),
        in_specs=[
            pl.BlockSpec(hot.shape, lambda d: (0, 0)),
            pl.BlockSpec(gate.shape, lambda d: (0, 0)),
        ]
        + [by_rows(block) for _ in blocks]
        + [by_rows(rows.shape[0]) for rows in arrived]
        + [pl.BlockSpec(memory_space=pl.ANY) for _ in wait_for],
        out_specs=[by_rows(n) for n in parts or (n_rows,)],
        out_shape=[jax.ShapeDtypeStruct((n, width), BF16) for n in parts or (n_rows,)],
        compiler_params=params(),
        cost_estimate=SHORT,
        name="combine",
    )(hot, gate, *blocks, *arrived, *wait_for)
    return results if parts else results[0]


def weight_kernel(n_dp, rows, traded_ref, pre_ref, hidden_ref, *outs):
    for i, factor_ref in enumerate((pre_ref, hidden_ref)):
        total = None
        for d in range(n_dp):
            part = contract_rows(
                traded_ref[d, i * rows : (i + 1) * rows, :],
                factor_ref[d * rows : (d + 1) * rows, :],
            )
            total = part if d == 0 else total + part
        outs[i][0] = total.astype(BF16)


def weight_grads(traded, pre_all, hidden_all, lanes):
    n_dp, depth, width = traded.shape
    hidden = pre_all.shape[1]
    whole = pl.BlockSpec(pre_all.shape, lambda i: (0, 0))
    return pl.pallas_call(
        functools.partial(weight_kernel, n_dp, depth // 2),
        grid=(width // lanes,),
        in_specs=[pl.BlockSpec((n_dp, depth, lanes), lambda i: (0, 0, i)), whole, whole],
        out_specs=[pl.BlockSpec((1, lanes, hidden), lambda i: (0, i, 0))] * 2,
        out_shape=[jax.ShapeDtypeStruct((1, width, hidden), BF16)] * 2,
        compiler_params=params(),
        cost_estimate=SHORT,
        name="weight_grads",
    )(traded, pre_all, hidden_all)


def after_kernel(*refs):
    pass


def after(values, *others):
    anywhere = pl.BlockSpec(memory_space=pl.ANY)
    return pl.pallas_call(
        after_kernel,
        in_specs=[anywhere] * (1 + len(others)),
        out_specs=anywhere,
        out_shape=jax.ShapeDtypeStruct(values.shape, values.dtype),
        input_output_aliases={0: 0},
        cost_estimate=SHORT,
        name="after",
    )(values, *others)


def permute_xor(values, axis, mask):
    size = lax.axis_size(axis)
    return lax.ppermute(values, axis, [(i, i ^ mask) for i in range(size)])


def exchange(blocks):
    return [blocks[0]] + [permute_xor(blocks[k], "expert", k) for k in range(1, len(blocks))]


def local(tokens, grad_out, expert_ids, gate_codes, w_up, w_down):
    n_expert = lax.axis_size("expert")
    n_dp = lax.axis_size("dp")
    n_rows, width = tokens.shape
    capacity = max(2, 12 * n_rows // (5 * n_expert))
    block = -(-capacity // ROW_TILE) * ROW_TILE
    half = n_expert // 2
    chunk = width // 2
    me = lax.axis_index("expert").astype(I32).reshape(1)

    def swap_direct(blocks):
        return lax.all_to_all(blocks, "expert", split_axis=0, concat_axis=0, tiled=True)

    routing = jnp.concatenate([expert_ids, gate_codes], axis=1)
    far_routing = permute_xor(routing, "expert", half)
    up_weight = lax.all_gather(w_up, "dp", axis=1, tiled=True)[0]
    down_weight = lax.all_gather(w_down, "dp", axis=1, tiled=True)[0]

    rows_out = dispatch(routing, tokens, n_expert, block, chunk)
    rows_in = swap_direct(rows_out)
    grads_out = dispatch(
        routing, grad_out, n_expert, block, chunk, gated=True, wait_for=(rows_out,)
    )
    grads_in = swap_direct(after(grads_out, far_routing))

    out, sent, hidden, pre_act = expert(me, rows_in, up_weight, down_weight, n_dp)
    parts = (5 * n_rows // 16, n_rows - 5 * n_rows // 16)
    far_out = exchange(out[half:])
    far_slots = plan(me, far_routing, half, block, (out[0],))
    near_slots = plan(me, routing, half, block, (out[0],))
    far_mixed = combine(far_slots, far_out, chunk, gated=True, parts=parts)
    near_back = exchange(out[:half])
    mixed_in = [permute_xor(far_mixed[0], "expert", half)]
    mixed_in.append(permute_xor(after(far_mixed[1], mixed_in[0]), "expert", half))

    row_grads, sent, pre_grad = expert(
        me, grads_in, down_weight, up_weight, n_dp, pre=pre_act, sent=sent, wait_for=far_mixed[0]
    )
    ready = (mixed_in[0], *near_back[1:])
    far_back = exchange([after(rows, *ready) for rows in row_grads[half:]])
    far_sum = combine(far_slots, far_back, chunk)
    sum_in = permute_xor(after(far_sum, mixed_in[1]), "expert", half)
    near_grad = exchange([after(rows, far_sum) for rows in row_grads[:half]])
    traded = lax.all_to_all(
        after(sent, *ready), "dp", split_axis=0, concat_axis=0, tiled=True
    )
    hidden_all = lax.all_gather(hidden, "dp", axis=0, tiled=True)
    pre_all = lax.all_gather(after(pre_grad, *ready), "dp", axis=0, tiled=True)

    grad_up, grad_down = weight_grads(traded, pre_all, hidden_all, 256)
    layer_output = combine(
        near_slots,
        near_back,
        chunk,
        gated=True,
        arrived=mixed_in,
        wait_for=(grad_up, grad_down),
    )
    grad_tokens = combine(
        near_slots, near_grad, chunk, arrived=(sum_in,), wait_for=(layer_output,)
    )
    return (layer_output, grad_tokens, grad_up, grad_down)


def solution(mesh):
    in_specs = (
        P(("dp", "expert"), None),
        P(("dp", "expert"), None),
        P(("dp", "expert"), None),
        P(("dp", "expert"), None),
        P("expert", "dp", None),
        P("expert", "dp", None),
    )
    out_specs = (
        P(("dp", "expert"), None),
        P(("dp", "expert"), None),
        P("expert", "dp", None),
        P("expert", "dp", None),
    )
    return jax.shard_map(local, mesh=mesh, in_specs=in_specs, out_specs=out_specs, check_vma=False)
```
